512 devices in a mesh: dp: 256 (over z, y, x), ctx: 2 (over core).
Axes of the slice: x: 4, y: 8, z: 8, core: 2. Of those that a mesh axis runs over, the one named last changes fastest.
Arguments:
- history: bfloat16 [256, 256, 512], P('dp', 'ctx'), may hold values from -6 to 6
- lengths: int32 [256], P('dp'), may hold values from 128 to 256, as said below
- input_gain: float32 [512], replicated, may hold values from 0.1 to 1.9
- gain_attn: float32 [512], replicated, may hold values from 0.1 to 1.9
- w_in: bfloat16 [512, 2048], replicated, may hold values from -0.25 to 0.25
- w_out: bfloat16 [512, 512], replicated, may hold values from -0.25 to 0.25
- cotangent: bfloat16 [256, 256, 512], P('dp', 'ctx'), may hold values from -6 to 6
Outputs:
- output: bfloat16 [256, 256, 512], P('dp', 'ctx')
- grad_history: bfloat16 [256, 256, 512], P('dp', 'ctx')
- grad_w_in: float32 [512, 2048], replicated
- grad_w_out: float32 [512, 512], replicated
- grad_gain_in: float32 [512], replicated
- grad_gain_attn: float32 [512], replicated
The draws below stay inside these ranges and needn't reach their ends.
Inputs may be any that keep to these rules, and one draw needn't show every extreme that they name: `lengths`: each length is a multiple of 128; some user has length 256 and another 128.
All inputs are finite; a program needn't handle non-finite values.
Results may differ from the reference program's by a relative error of at most 0.0088.
Values may be sent and summed in bfloat16 or wider, within the bound.
A program may use at most 64 MiB of HBM per device.

```python
import math
import jax
import jax.numpy as jnp
from jax import lax

D = 512
H = 8
DH = 64
BLK = 128
SEQ = 256
USERS = 256


def draw_lengths(key, part):
    key = jax.random.fold_in(key, 7)
    key_count, key_long, key_short = jax.random.split(key, 3)
    blocks = SEQ // BLK
    counts = jax.random.randint(key_count, (USERS,), 1, blocks + 1)
    longest = jax.random.randint(key_long, (), 0, USERS)
    shortest = (longest + 1 + jax.random.randint(key_short, (), 0, USERS - 1)) % USERS
    slots = jnp.arange(USERS)
    counts = jnp.where(slots == longest, blocks, counts)
    counts = jnp.where(slots == shortest, 1, counts)
    return (counts * BLK).astype(jnp.int32)


def block_scale(own_key, dims, pieces, least, top_value):
    factor_of, own = 1.0, jax.random.fold_in(own_key, 6)
    for dim, shards_of in pieces:
        heights = jnp.exp(jax.random.uniform(jax.random.fold_in(own, dim), (shards_of,), jnp.float32, least / len(pieces), top_value / len(pieces)))
        factor_of = factor_of * jnp.repeat(heights, dims[dim] // shards_of).reshape([-1 if axis == dim else 1 for axis in range(len(dims))])
    return factor_of


def centred(own_key, shape, scale, reach, shards=(), kind=jnp.bfloat16):
    entries = scale * jax.random.normal(own_key, shape, jnp.float32)
    if shards:
        entries = entries * block_scale(own_key, shape, shards, -0.22, 0.18)
    return jnp.clip(entries, -reach, reach).astype(kind)


def setup_inputs(seed: int = 0) -> dict:
    keys = jax.random.split(jax.random.key(seed), 8)
    history = centred(keys[0], (USERS, SEQ, D), 1.0, 6.0, ((0, 256), (1, 2)))
    lengths = draw_lengths(jax.random.fold_in(keys[7], 71), 0)
    input_gain = jnp.clip(1.0 + 0.18 * jax.random.normal(keys[2], (D,), jnp.float32), 0.1, 1.9)
    gain_attn = jnp.clip(1.0 + 0.18 * jax.random.normal(keys[3], (D,), jnp.float32), 0.1, 1.9)
    w_in = centred(keys[4], (D, 4 * D), D ** -0.5, 0.25)
    w_out = centred(keys[5], (D, D), D ** -0.5, 0.25)
    cotangent = centred(keys[6], (USERS, SEQ, D), 1.0, 6.0, ((0, 256), (1, 2)))
    return dict(history=history, lengths=lengths, input_gain=input_gain, gain_attn=gain_attn, w_in=w_in, w_out=w_out, cotangent=cotangent)


EPS = 1e-05

def apply_rms_norm(tensor):
    mean = lax.optimization_barrier(jnp.mean(tensor, axis=-1, keepdims=True))
    centered = tensor - mean
    variance = lax.optimization_barrier(jnp.mean(centered * centered, axis=-1, keepdims=True))
    rstd = lax.rsqrt(variance + EPS)
    return (centered * rstd, rstd)

def norm_backward_pass(grad, normed, rstd):
    return rstd * (grad - lax.optimization_barrier(jnp.mean(grad, axis=-1, keepdims=True)) - normed * lax.optimization_barrier(jnp.mean(grad * normed, axis=-1, keepdims=True)))

def silu_slope(tensor):
    sigmoid_v = jax.nn.sigmoid(tensor)
    return sigmoid_v * (1.0 + tensor * (1.0 - sigmoid_v))

def round_bf16(tensor):
    return lax.optimization_barrier(tensor.astype(jnp.bfloat16)).astype(jnp.float32)

def one_user(history_row, cot_row, length, input_gain, gain_attn, w_in, w_out):
    score_scale = 1.0 / math.sqrt(DH)
    inputs_float = history_row.astype(jnp.float32)
    standardized_input, input_inverse_deviation = apply_rms_norm(inputs_float)
    normalized_input = (standardized_input * input_gain).astype(jnp.bfloat16)
    pre_act = jnp.dot(normalized_input, w_in, preferred_element_type=jnp.float32)
    hidden = round_bf16(jax.nn.silu(pre_act))
    gating = hidden[:, :D]
    value_rows = hidden[:, D:2 * D].reshape(SEQ, H, DH)
    query_rows = hidden[:, 2 * D:3 * D].reshape(SEQ // BLK, BLK, H, DH)
    key_rows = hidden[:, 3 * D:].reshape(SEQ, H, DH)
    positions = jnp.arange(SEQ, dtype=jnp.int32)
    query_pos = positions.reshape(SEQ // BLK, BLK)

    def block_scores(q_block, q_pos):
        scores = jnp.einsum('qhd,khd->hqk', q_block, key_rows) * score_scale
        pair_mask = ((positions[None, :] <= q_pos[:, None]) & (q_pos[:, None] < length)).astype(jnp.float32)
        return (scores, pair_mask)

    def forward_block(carry, inputs):
        q_block, q_pos = inputs
        scores, pair_mask = block_scores(q_block, q_pos)
        weights = round_bf16(jax.nn.silu(scores) * pair_mask)
        attended = jnp.einsum('hqk,khd->qhd', weights, value_rows).reshape(BLK, D)
        return (carry, attended)
    _, attended = lax.scan(forward_block, jnp.zeros((), jnp.float32), (query_rows, query_pos))
    attended = attended.reshape(SEQ, D)
    normed, rstd_attn = apply_rms_norm(attended)
    mixed = (normed * gain_attn * gating).astype(jnp.bfloat16)
    valid = (positions < length).astype(jnp.float32)[:, None]
    proj = jnp.dot(mixed, w_out, preferred_element_type=jnp.float32)
    output = (inputs_float + valid * proj).astype(jnp.bfloat16)
    cot_f = cot_row.astype(jnp.float32)
    d_proj = (cot_f * valid).astype(jnp.bfloat16)
    g_out = jnp.dot(mixed.T, d_proj, preferred_element_type=jnp.float32)
    d_mixed = jnp.dot(d_proj, w_out.T, preferred_element_type=jnp.float32)
    d_gating = d_mixed * normed * gain_attn
    g_attn = lax.optimization_barrier(jnp.sum(d_mixed * normed * gating, axis=0))
    d_att = round_bf16(norm_backward_pass(d_mixed * gain_attn * gating, normed, rstd_attn))
    d_blocks = d_att.reshape(SEQ // BLK, BLK, H, DH)

    def backward_block(carry, inputs):
        d_keys, d_values = carry
        q_block, q_pos, d_block = inputs
        scores, pair_mask = block_scores(q_block, q_pos)
        weights = round_bf16(jax.nn.silu(scores) * pair_mask)
        pair_grads = jnp.einsum('qhd,khd->hqk', d_block, value_rows)
        slopes = round_bf16(pair_grads * silu_slope(scores) * pair_mask)
        d_query = jnp.einsum('hqk,khd->qhd', slopes, key_rows).reshape(BLK, D) * score_scale
        d_keys = d_keys + jnp.einsum('hqk,qhd->khd', slopes, q_block).reshape(SEQ, D) * score_scale
        d_values = d_values + jnp.einsum('hqk,qhd->khd', weights, d_block).reshape(SEQ, D)
        return ((d_keys, d_values), d_query)
    zero_full = jnp.zeros((SEQ, D), jnp.float32)
    (d_keys, d_values), d_query = lax.scan(backward_block, (zero_full, zero_full), (query_rows, query_pos, d_blocks))
    d_query = d_query.reshape(SEQ, D)
    d_hidden = jnp.concatenate([d_gating, d_values, d_query, d_keys], axis=1)
    d_pre = (d_hidden * silu_slope(pre_act)).astype(jnp.bfloat16)
    g_in = jnp.dot(normalized_input.T, d_pre, preferred_element_type=jnp.float32)
    normed_gradient = jnp.dot(d_pre, w_in.T, preferred_element_type=jnp.float32)
    input_gain_gradient = lax.optimization_barrier(jnp.sum(normed_gradient * standardized_input, axis=0))
    input_gradient = norm_backward_pass(normed_gradient * input_gain, standardized_input, input_inverse_deviation)
    grad_row = (cot_f + input_gradient).astype(jnp.bfloat16)
    return (output, grad_row, g_in, g_out, input_gain_gradient, g_attn)

def reference(history, lengths, input_gain, gain_attn, w_in, w_out, cotangent):

    def per_user(carry, inputs):
        history_row, cot_row, length = inputs
        output, grad_row, g_in, g_out, input_gain_gradient, g_attn = one_user(history_row, cot_row, length, input_gain, gain_attn, w_in, w_out)
        carry = jax.tree.map(jnp.add, carry, (g_in, g_out, input_gain_gradient, g_attn))
        return (carry, (output, grad_row))
    start_sums = (jnp.zeros((D, 4 * D), jnp.float32), jnp.zeros((D, D), jnp.float32), jnp.zeros((D,), jnp.float32), jnp.zeros((D,), jnp.float32))
    sums, (outputs, grads) = lax.scan(per_user, start_sums, (history, cotangent, lengths))
    factor = 1.0 / math.sqrt(USERS * SEQ)
    return (outputs, grads, sums[0] * factor, sums[1] * factor, sums[2] * factor, sums[3] * factor)
```

```python
import functools
import math

import jax
import jax.numpy as jnp
from jax import lax
from jax.experimental import pallas as pl
from jax.experimental.pallas import tpu as pltpu
from jax.sharding import PartitionSpec as P

MESH = pl.DeviceIdType.MESH
F32 = jnp.float32
BF16 = jnp.bfloat16
D = 512
DH = 64
BLK = 128
SEQ = 256
HALF = 256
HEADS = 4
SIZES = (4, 8, 8)
EPS = 1e-05
SCORE_SCALE = 1.0 / math.sqrt(DH)
XYZ, XZY, YXZ, ZXY = (0, 1, 2), (0, 2, 1), (1, 0, 2), (2, 0, 1)
STREAMS = (
    (XYZ, 32),
    (XZY, 32),
    (XYZ, 16),
    (XZY, 16),
    (XYZ, 16),
    (XZY, 16),
    (YXZ, 16),
    (ZXY, 16),
)
LEVELS = 5


def dot(left, right, dims):
    return lax.dot_general(left, right, (dims, ((), ())), preferred_element_type=F32)


def rows_dot(left, right):
    return dot(left, right, ((1,), (0,)))


def cols_dot(left, right):
    return dot(left, right, ((1,), (1,)))


def sum_rows_dot(left, right):
    return dot(left, right, ((0,), (0,)))


def sigmoid(t):
    return 0.5 * jnp.tanh(0.5 * t) + 0.5


def standardize(t):
    centered = t - jnp.mean(t, axis=-1, keepdims=True)
    rstd = lax.rsqrt(jnp.mean(centered * centered, axis=-1, keepdims=True) + EPS)
    return centered * rstd, rstd


class Place:
    def __init__(self):
        self.dp = lax.axis_index("dp")
        self.core = lax.axis_index("ctx")
        self.pos = (lax.rem(self.dp, 4), lax.rem(self.dp // 4, 8), self.dp // 32)

    def device(self, axis, index):
        q = list(self.pos)
        q[axis] = index
        return ((q[2] * 8 + q[1]) * 4 + q[0], self.core)

    def partner(self):
        return (self.dp, 1 - self.core)


def wait_bytes(region, sem):
    pltpu.make_async_copy(region, region, sem).wait()


class Stream:
    def __init__(self, place, order, bufs, result, ssem, rsem, base):
        self.place, self.order, self.base = place, order, base
        self.src, self.r1, self.s1, self.r2, self.r3 = bufs
        self.res = result
        self.ssem, self.rsem = ssem, rsem
        self.n = [SIZES[a] for a in order]
        self.me = [place.pos[a] for a in order]

    def fan(self, phase, level, src, dst):
        n, me = self.n[level], self.me[level]
        for d in sorted(range(1, n), key=lambda d: -min(d, n - d)):
            k = lax.rem(me + d, n)
            pltpu.make_async_remote_copy(
                src_ref=src(k),
                dst_ref=dst,
                send_sem=self.ssem.at[self.base + phase],
                recv_sem=self.rsem.at[self.base + phase],
                device_id=self.place.device(self.order[level], k),
                device_id_type=MESH,
            ).start()

    def wait_recv(self, phase, region):
        wait_bytes(region, self.rsem.at[self.base + phase])

    def total(self, ref, n):
        acc = ref[0].astype(F32)
        for j in range(1, n):
            acc = acc + ref[j].astype(F32)
        return acc.astype(BF16)

    def scatter1(self):
        self.fan(0, 0, lambda k: self.src.at[k], self.r1.at[self.me[0]])

    def scatter2(self):
        n, me = self.n[0], self.me[0]
        self.wait_recv(0, self.r1.at[pl.ds(0, n - 1)])
        self.r1[me] = self.src[me]
        self.s1[...] = self.total(self.r1, n)
        self.fan(1, 1, lambda k: self.s1.at[k], self.r2.at[self.me[1]])

    def exchange(self):
        n, me = self.n[1], self.me[1]
        self.wait_recv(1, self.r2.at[pl.ds(0, n - 1)])
        self.r2[me] = self.s1[me]
        own = self.r3.at[self.me[2]]
        own[...] = self.total(self.r2, n)
        self.fan(2, 2, lambda k: own, own)

    def gather2(self):
        n = self.n[2]
        self.wait_recv(2, self.r3.at[pl.ds(0, n - 1)])
        own = self.res.at[self.me[0], self.me[1]]
        own[...] = self.total(self.r3, n)
        self.fan(3, 1, lambda k: own, own)

    def gather1(self):
        own = self.res.at[self.me[0]]
        self.wait_recv(3, own.at[pl.ds(0, self.n[1] - 1)])
        self.fan(4, 0, lambda k: own, own)

    def finish(self):
        self.wait_recv(4, self.res.at[pl.ds(0, self.n[0] - 1)])

    def drain(self):
        n = self.n
        regions = (
            self.r1.at[pl.ds(0, n[0] - 1)],
            self.r2.at[pl.ds(0, n[1] - 1)],
            self.r3.at[pl.ds(0, n[2] - 1)],
            self.res.at[0, pl.ds(0, n[1] - 1)],
            self.res.at[pl.ds(0, n[0] - 1)],
        )
        for phase, region in enumerate(regions):
            wait_bytes(region, self.ssem.at[self.base + phase])


def share_kernel(hist_ref, cot_ref, gain_ref, normed_ref, cots_ref, ssem, rsem):
    place = Place()
    core = place.core
    barrier = pltpu.get_barrier_semaphore()
    pl.semaphore_signal(barrier, inc=1, device_id=place.partner(), device_id_type=MESH)
    xhat, _ = standardize(hist_ref[...].astype(F32))
    normed_ref[core] = (xhat * gain_ref[...]).astype(BF16)
    cots_ref[core] = cot_ref[...]
    pl.semaphore_wait(barrier, 1)
    copies = []
    for i, ref in enumerate((cots_ref, normed_ref)):
        copies.append(
            pltpu.make_async_remote_copy(
                src_ref=ref.at[core],
                dst_ref=ref.at[core],
                send_sem=ssem.at[i],
                recv_sem=rsem.at[i],
                device_id=place.partner(),
                device_id_type=MESH,
            )
        )
        copies[-1].start()
    for copy in copies:
        copy.wait()


def layer_kernel(
    len_ref, hist_ref, normed_ref, cots_ref, gain_in_ref, gain_attn_ref, w_in_ref, w_out_ref,
    out_ref, grad_ref, gains_ref, *rest,
):
    ns = len(STREAMS)
    results, rest = rest[:ns], rest[ns:]
    stream_bufs, rest = rest[: 5 * ns], rest[5 * ns :]
    (
        w_own, wo_own, hid, slope, weights, turn, slopes, dpre, stat_own, stat_other, proj, proj_in, dnorm, dnorm_in,
        gx0, gx1, gx2, gx3,
        wsem, ssem, rsem, psem, qsem, gssem, grsem, fssem, frsem,
    ) = rest
    place = Place()
    core = place.core
    partner = place.partner()

    barrier = pltpu.get_barrier_semaphore()
    for axis, n in enumerate(SIZES):
        for d in range(1, n):
            pl.semaphore_signal(
                barrier,
                inc=1,
                device_id=place.device(axis, lax.rem(place.pos[axis] + d, n)),
                device_id_type=MESH,
            )
    pl.semaphore_signal(barrier, inc=1, device_id=partner, device_id_type=MESH)

    first = pl.multiple_of(core * HALF, HALF)
    loads = []
    for g in range(4):
        loads.append(
            pltpu.make_async_copy(
                w_in_ref.at[:, pl.ds(pl.multiple_of(g * D + first, HALF), HALF)], w_own.at[g], wsem.at[g]
            )
        )
    loads.append(pltpu.make_async_copy(w_out_ref.at[pl.ds(first, HALF), :], wo_own, wsem.at[4]))
    for load in loads:
        load.start()

    streams = [
        Stream(place, order, stream_bufs[5 * i : 5 * i + 5], results[i].at[core], ssem, rsem, LEVELS * i)
        for i, (order, _) in enumerate(STREAMS)
    ]

    def to_partner(src, dst, i):
        copy = pltpu.make_async_remote_copy(
            src_ref=src,
            dst_ref=dst,
            send_sem=psem.at[i],
            recv_sem=qsem.at[i],
            device_id=partner,
            device_id_type=MESH,
        )
        copy.start()
        return copy

    length = len_ref[0]
    row = lax.broadcasted_iota(jnp.int32, (SEQ, 1), 0)
    valid = (row < length).astype(F32)
    normed = normed_ref[...].reshape(SEQ, D)
    d_proj = (cots_ref[...].reshape(SEQ, D).astype(F32) * valid).astype(BF16)
    gain_attn = gain_attn_ref[:, pl.ds(first, HALF)]

    for g in (2, 3, 1, 0):
        loads[g].wait()
        pre = rows_dot(normed, w_own[g])
        sig = sigmoid(pre)
        hid[g] = (pre * sig).astype(BF16)
        slope[g] = sig * (1.0 + pre * (1.0 - sig))
    q_pos = lax.broadcasted_iota(jnp.int32, (SEQ, SEQ), 0)
    k_pos = lax.broadcasted_iota(jnp.int32, (SEQ, SEQ), 1)
    mask = ((k_pos <= q_pos) & (q_pos < length)).astype(F32)
    lane_head = lax.broadcasted_iota(jnp.int32, (1, HALF), 1) // DH

    def of_head(t, h):
        return jnp.where(lane_head == h, t, jnp.zeros_like(t))

    query, key, value = hid[2], hid[3], hid[1]
    attended = jnp.zeros((SEQ, HALF), F32)
    for h in range(HEADS):
        scores = cols_dot(of_head(query, h), key) * SCORE_SCALE
        sig = sigmoid(scores)
        weight = (scores * sig * mask).astype(BF16)
        weights[h] = weight
        turn[h] = sig * (1.0 + scores * (1.0 - sig)) * mask
        attended = attended + rows_dot(weight, of_head(value, h))

    loads[4].wait()
    gating = hid[0].astype(F32)
    d_mixed = cols_dot(d_proj, wo_own[...])
    g = d_mixed * gain_attn * gating
    half_mean = jnp.mean(attended, axis=-1, keepdims=True)
    centered = attended - half_mean
    half_sq = jnp.sum(centered * centered, axis=-1, keepdims=True)
    half_g = jnp.sum(g, axis=-1, keepdims=True)
    half_gc = jnp.sum(g * centered, axis=-1, keepdims=True)
    lane = lax.broadcasted_iota(jnp.int32, (SEQ, 128), 1)
    stat_own[...] = jnp.where(
        lane == 0, half_mean, jnp.where(lane == 1, half_sq, jnp.where(lane == 2, half_g, half_gc))
    )
    pl.semaphore_wait(barrier, 18)
    stat_copy = to_partner(stat_own, stat_other, 0)
    stat_copy.wait()
    other = stat_other[...]
    o_mean, o_sq, o_g, o_gc = (other[:, i : i + 1] for i in range(4))
    mean = 0.5 * (half_mean + o_mean)
    up, o_up = half_mean - mean, o_mean - mean
    var = (half_sq + o_sq + HALF * (up * up + o_up * o_up)) * (1.0 / D)
    rstd = lax.rsqrt(var + EPS)
    mean_g = (half_g + o_g) * (1.0 / D)
    mean_gn = rstd * (half_gc + o_gc + half_g * up + o_g * o_up) * (1.0 / D)
    norm = (attended - mean) * rstd
    ng = norm * gain_attn
    mixed = (ng * gating).astype(BF16)
    d_att = (rstd * (g - mean_g - norm * mean_gn)).astype(BF16)
    g_attn = jnp.sum(d_mixed * norm * gating, axis=0, keepdims=True)

    def put(stream, first_row, rows, part):
        n = streams[stream].n
        streams[stream].src[:, :, first_row : first_row + rows, :] = part.astype(BF16).reshape(n[0], n[1], rows, 128)

    def weight_grad(g, d_hidden):
        d_pre = (d_hidden * slope[g]).astype(BF16)
        dpre[g] = d_pre
        return sum_rows_dot(normed, d_pre)

    g_u = weight_grad(0, d_mixed * ng)
    g_out = sum_rows_dot(mixed, d_proj)
    for half in range(2):
        put(half, 0, 16, g_u[:, half * 128 : half * 128 + 128])
        blocks = [g_out[:, (2 * half + i) * 128 : (2 * half + i) * 128 + 128] for i in range(2)]
        put(half, 16, 16, jnp.concatenate(blocks, axis=0))
        streams[half].scatter1()

    d_values = jnp.zeros((SEQ, HALF), F32)
    for h in range(HEADS):
        d_att_h = of_head(d_att, h)
        d_values = d_values + sum_rows_dot(weights[h], d_att_h)
    g_v = weight_grad(1, d_values)
    for half in range(2):
        put(2 + half, 0, 16, g_v[:, half * 128 : half * 128 + 128])
        streams[2 + half].scatter1()

    d_query = jnp.zeros((SEQ, HALF), F32)
    d_keys = jnp.zeros((SEQ, HALF), F32)
    for h in range(HEADS):
        pair_grads = cols_dot(of_head(d_att, h), value)
        slopes_h = (pair_grads * turn[h]).astype(BF16)
        d_query = d_query + rows_dot(slopes_h, of_head(key, h))
        d_keys = d_keys + sum_rows_dot(slopes_h, of_head(query, h))
    g_q = weight_grad(2, d_query * SCORE_SCALE)
    for half in range(2):
        put(4 + half, 0, 16, g_q[:, half * 128 : half * 128 + 128])
        streams[4 + half].scatter1()
    g_k = weight_grad(3, d_keys * SCORE_SCALE)
    for half in range(2):
        put(6 + half, 0, 16, g_k[:, half * 128 : half * 128 + 128])
        streams[6 + half].scatter1()

    d_norm = cols_dot(dpre[0], w_own[0])
    for g in range(1, 4):
        d_norm = d_norm + cols_dot(dpre[g], w_own[g])
    dnorm[...] = d_norm.reshape(2, BLK, D)
    dnorm_copy = to_partner(dnorm.at[1 - core], dnorm_in, 1)
    for s in streams[:2]:
        s.scatter2()
    proj[...] = rows_dot(mixed, wo_own[...]).reshape(2, BLK, D)
    proj_copy = to_partner(proj.at[1 - core], proj_in, 2)

    history = hist_ref[...].astype(F32)
    xhat, rstd_in = standardize(history)
    dnorm_copy.wait()
    d_norm = dnorm[core] + dnorm_in[...]
    gain_part = jnp.sum(d_norm * xhat, axis=0, keepdims=True)

    mine = (core == 0).astype(F32)
    gx0_own = gx0.at[core]
    for i in range(4):
        gx0_own[i : i + 1, :] = gain_part[:, i * 128 : i * 128 + 128]
    for i in range(2):
        part = g_attn[:, i * 128 : i * 128 + 128]
        gx0_own[4 + i : 5 + i, :] = part * mine
        gx0_own[6 + i : 7 + i, :] = part * (1.0 - mine)
    gain_copy = to_partner(gx0_own, gx0_own, 3)

    def gains_fan(axis, buf):
        n, me = SIZES[axis], place.pos[axis]
        own = buf.at[me]
        for d in range(1, n):
            pltpu.make_async_remote_copy(
                src_ref=own,
                dst_ref=own,
                send_sem=gssem.at[axis],
                recv_sem=grsem.at[axis],
                device_id=place.device(axis, lax.rem(me + d, n)),
                device_id_type=MESH,
            ).start()

    def gains_total(axis, buf):
        n = SIZES[axis]
        wait_bytes(buf.at[pl.ds(0, n - 1)], grsem.at[axis])
        acc = buf[0]
        for j in range(1, n):
            acc = acc + buf[j]
        return acc

    for s in streams[2:4]:
        s.scatter2()
    gain_copy.wait()
    gx1[place.pos[0]] = gx0[0] + gx0[1]
    gains_fan(0, gx1)
    for s in streams[4:]:
        s.scatter2()

    e = d_norm * gain_in_ref[...]
    d_hist = rstd_in * (
        e - jnp.mean(e, axis=-1, keepdims=True) - xhat * jnp.mean(e * xhat, axis=-1, keepdims=True)
    )
    grad_ref[...] = (cots_ref[core].astype(F32) + d_hist).astype(BF16)
    proj_copy.wait()
    own_row = lax.broadcasted_iota(jnp.int32, (BLK, 1), 0) + core * BLK
    own_valid = (own_row < length).astype(F32)
    out_ref[...] = (history + own_valid * (proj[core] + proj_in[...])).astype(BF16)

    for s in streams[:4]:
        s.exchange()
    gx2[place.pos[1]] = gains_total(0, gx1)
    gains_fan(1, gx2)
    for s in streams[4:]:
        s.exchange()
    for s in streams[:4]:
        s.gather2()
    gx3[place.pos[2]] = gains_total(1, gx2)
    gains_fan(2, gx3)
    for s in streams[4:]:
        s.gather2()
    for s in streams:
        s.gather1()
    gains_ref[...] = gains_total(2, gx3)
    forwards = []
    for i, s in enumerate(streams):
        s.finish()
        forwards.append(
            pltpu.make_async_remote_copy(
                src_ref=s.res,
                dst_ref=s.res,
                send_sem=fssem.at[i],
                recv_sem=frsem.at[i],
                device_id=partner,
                device_id_type=MESH,
            )
        )
        forwards[-1].start()
    for axis, buf in enumerate((gx1, gx2, gx3)):
        wait_bytes(buf.at[pl.ds(0, SIZES[axis] - 1)], gssem.at[axis])
    for s in streams:
        s.drain()
    for copy in forwards:
        copy.wait()


def widen_kernel(factor, *refs):
    ns = len(STREAMS)
    gains_ref, results = refs[0], refs[1 : 1 + ns]
    w_in_ref, w_out_ref, gin_ref, gattn_ref = refs[1 + ns :]

    def wide(t):
        return t.astype(F32) * factor

    for g in range(4):
        for half in range(2):
            res = results[2 * g + half]
            for core in range(2):
                column = (4 * g + 2 * core + half) * 128
                part = res[core, :, :, 0:16, :].reshape(D, 128)
                w_in_ref[:, column : column + 128] = wide(part)
    for half in range(2):
        for core in range(2):
            part = wide(results[half][core, :, :, 16:32, :].reshape(D, 128))
            for i in range(2):
                column = (2 * half + i) * 128
                w_out_ref[core * HALF : core * HALF + HALF, column : column + 128] = part[i * HALF : i * HALF + HALF]
    for i in range(4):
        gin_ref[:, i * 128 : i * 128 + 128] = gains_ref[i : i + 1, :] * factor
        gattn_ref[:, i * 128 : i * 128 + 128] = gains_ref[4 + i : 5 + i, :] * factor


VMEM = pl.BlockSpec(memory_space=pltpu.VMEM)
SMEM = pl.BlockSpec(memory_space=pltpu.SMEM)
ANY = pl.BlockSpec(memory_space=pl.ANY)


def shape(dims, kind):
    return jax.ShapeDtypeStruct(dims, kind)


def per_device(users, history, lengths, input_gain, gain_attn, w_in, w_out, cotangent):
    history, cotangent = history[0], cotangent[0]
    input_gain, gain_attn = input_gain[None], gain_attn[None]
    dma = pltpu.SemaphoreType.DMA
    normed, cots = pl.pallas_call(
        share_kernel,
        out_shape=(shape((2, BLK, D), BF16),) * 2,
        in_specs=[VMEM] * 3,
        out_specs=(VMEM,) * 2,
        scratch_shapes=[dma((2,)), dma((2,))],
        compiler_params=pltpu.CompilerParams(collective_id=1, has_side_effects=True, vmem_limit_bytes=8 << 20),
        name="share",
    )(history, cotangent, input_gain)

    buffers, result_shapes = [], []
    for order, rows in STREAMS:
        n = [SIZES[a] for a in order]
        result_shapes.append(shape((2, n[0], n[1], rows, 128), BF16))
        buffers += [
            pltpu.VMEM((n[0], n[1], rows, 128), BF16),
            pltpu.VMEM((n[0], n[1], rows, 128), BF16),
            pltpu.VMEM((n[1], rows, 128), BF16),
            pltpu.VMEM((n[1], rows, 128), BF16),
            pltpu.VMEM((n[2], rows, 128), BF16),
        ]
    ns = len(STREAMS)
    out, grad, gains, *results = pl.pallas_call(
        layer_kernel,
        out_shape=(shape((BLK, D), BF16), shape((BLK, D), BF16), shape((8, 128), F32), *result_shapes),
        in_specs=[SMEM, VMEM, VMEM, VMEM, VMEM, VMEM, ANY, ANY],
        out_specs=(VMEM,) * (3 + ns),
        scratch_shapes=buffers
        + [
            pltpu.VMEM((4, D, HALF), BF16),
            pltpu.VMEM((HALF, D), BF16),
            pltpu.VMEM((4, SEQ, HALF), BF16),
            pltpu.VMEM((4, SEQ, HALF), F32),
            pltpu.VMEM((HEADS, SEQ, SEQ), BF16),
            pltpu.VMEM((HEADS, SEQ, SEQ), F32),
            pltpu.VMEM((HEADS, SEQ, SEQ), BF16),
            pltpu.VMEM((4, SEQ, HALF), BF16),
            pltpu.VMEM((SEQ, 128), F32),
            pltpu.VMEM((SEQ, 128), F32),
            pltpu.VMEM((2, BLK, D), F32),
            pltpu.VMEM((BLK, D), F32),
            pltpu.VMEM((2, BLK, D), F32),
            pltpu.VMEM((BLK, D), F32),
            pltpu.VMEM((2, 8, 128), F32),
            pltpu.VMEM((4, 8, 128), F32),
            pltpu.VMEM((8, 8, 128), F32),
            pltpu.VMEM((8, 8, 128), F32),
            dma((5,)),
            dma((LEVELS * ns,)),
            dma((LEVELS * ns,)),
            dma((4,)),
            dma((4,)),
            dma((3,)),
            dma((3,)),
            dma((ns,)),
            dma((ns,)),
        ],
        compiler_params=pltpu.CompilerParams(collective_id=2, has_side_effects=True, vmem_limit_bytes=48 << 20),
        name="layer",
    )(lengths, history, normed, cots, input_gain, gain_attn, w_in, w_out)

    factor = 1.0 / math.sqrt(users * SEQ)
    g_in, g_out, gain_in_grad, gain_attn_grad = pl.pallas_call(
        functools.partial(widen_kernel, factor),
        out_shape=(shape((D, 4 * D), F32), shape((D, D), F32), shape((1, D), F32), shape((1, D), F32)),
        in_specs=[VMEM] * (1 + ns),
        out_specs=(VMEM,) * 4,
        compiler_params=pltpu.CompilerParams(vmem_limit_bytes=32 << 20),
        name="widen",
    )(gains, *results)
    return out[None], grad[None], g_in, g_out, gain_in_grad[0], gain_attn_grad[0]


def solution(mesh):
    placed = (P("dp", "ctx", None), P("dp"), P(), P(), P(), P(), P("dp", "ctx", None))
    return jax.shard_map(
        functools.partial(per_device, mesh.shape["dp"]),
        mesh=mesh,
        in_specs=placed,
        out_specs=(P("dp", "ctx", None), P("dp", "ctx", None), P(), P(), P(), P()),
        check_vma=False,
    )
```

```python
import functools
import math

import jax
import jax.numpy as jnp
from jax import lax
from jax.experimental import pallas as pl
from jax.experimental.pallas import tpu as pltpu
from jax.sharding import PartitionSpec as P

MESH = pl.DeviceIdType.MESH
F32 = jnp.float32
BF16 = jnp.bfloat16
D = 512
DH = 64
BLK = 128
SEQ = 256
HALF = 256
HEADS = 4
SIZES = (4, 8, 8)
EPS = 1e-05
SCORE_SCALE = 1.0 / math.sqrt(DH)
XYZ, XZY, YXZ, ZXY = (0, 1, 2), (0, 2, 1), (1, 0, 2), (2, 0, 1)
STREAMS = (
    (XYZ, 32),
    (XZY, 32),
    (XYZ, 16),
    (XZY, 16),
    (XYZ, 16),
    (XZY, 16),
    (YXZ, 16),
    (ZXY, 16),
)
LEVELS = 5


def dot(left, right, dims):
    return lax.dot_general(left, right, (dims, ((), ())), preferred_element_type=F32)


def rows_dot(left, right):
    return dot(left, right, ((1,), (0,)))


def cols_dot(left, right):
    return dot(left, right, ((1,), (1,)))


def sum_rows_dot(left, right):
    return dot(left, right, ((0,), (0,)))


def sigmoid(t):
    return 0.5 * jnp.tanh(0.5 * t) + 0.5


def standardize(t):
    centered = t - jnp.mean(t, axis=-1, keepdims=True)
    rstd = lax.rsqrt(jnp.mean(centered * centered, axis=-1, keepdims=True) + EPS)
    return centered * rstd, rstd


class Place:
    def __init__(self):
        self.dp = lax.axis_index("dp")
        self.core = lax.axis_index("ctx")
        self.pos = (lax.rem(self.dp, 4), lax.rem(self.dp // 4, 8), self.dp // 32)

    def device(self, axis, index):
        q = list(self.pos)
        q[axis] = index
        return ((q[2] * 8 + q[1]) * 4 + q[0], self.core)

    def partner(self):
        return (self.dp, 1 - self.core)


def wait_bytes(region, sem):
    pltpu.make_async_copy(region, region, sem).wait()


class Stream:
    def __init__(self, place, order, bufs, result, ssem, rsem, base):
        self.place, self.order, self.base = place, order, base
        self.src, self.r1, self.s1, self.r2, self.r3 = bufs
        self.res = result
        self.ssem, self.rsem = ssem, rsem
        self.n = [SIZES[a] for a in order]
        self.me = [place.pos[a] for a in order]

    def fan(self, phase, level, src, dst):
        n, me = self.n[level], self.me[level]
        for d in sorted(range(1, n), key=lambda d: -min(d, n - d)):
            k = lax.rem(me + d, n)
            pltpu.make_async_remote_copy(
                src_ref=src(k),
                dst_ref=dst,
                send_sem=self.ssem.at[self.base + phase],
                recv_sem=self.rsem.at[self.base + phase],
                device_id=self.place.device(self.order[level], k),
                device_id_type=MESH,
            ).start()

    def wait_recv(self, phase, region):
        wait_bytes(region, self.rsem.at[self.base + phase])

    def total(self, ref, n):
        acc = ref[0].astype(F32)
        for j in range(1, n):
            acc = acc + ref[j].astype(F32)
        return acc.astype(BF16)

    def scatter1(self):
        self.fan(0, 0, lambda k: self.src.at[k], self.r1.at[self.me[0]])

    def scatter2(self):
        n, me = self.n[0], self.me[0]
        self.wait_recv(0, self.r1.at[pl.ds(0, n - 1)])
        self.r1[me] = self.src[me]
        self.s1[...] = self.total(self.r1, n)
        self.fan(1, 1, lambda k: self.s1.at[k], self.r2.at[self.me[1]])

    def exchange(self):
        n, me = self.n[1], self.me[1]
        self.wait_recv(1, self.r2.at[pl.ds(0, n - 1)])
        self.r2[me] = self.s1[me]
        own = self.r3.at[self.me[2]]
        own[...] = self.total(self.r2, n)
        self.fan(2, 2, lambda k: own, own)

    def gather2(self):
        n = self.n[2]
        self.wait_recv(2, self.r3.at[pl.ds(0, n - 1)])
        own = self.res.at[self.me[0], self.me[1]]
        own[...] = self.total(self.r3, n)
        self.fan(3, 1, lambda k: own, own)

    def gather1(self):
        own = self.res.at[self.me[0]]
        self.wait_recv(3, own.at[pl.ds(0, self.n[1] - 1)])
        self.fan(4, 0, lambda k: own, own)

    def finish(self):
        self.wait_recv(4, self.res.at[pl.ds(0, self.n[0] - 1)])

    def drain(self):
        n = self.n
        regions = (
            self.r1.at[pl.ds(0, n[0] - 1)],
            self.r2.at[pl.ds(0, n[1] - 1)],
            self.r3.at[pl.ds(0, n[2] - 1)],
            self.res.at[0, pl.ds(0, n[1] - 1)],
            self.res.at[pl.ds(0, n[0] - 1)],
        )
        for phase, region in enumerate(regions):
            wait_bytes(region, self.ssem.at[self.base + phase])


def layer_kernel(
    len_ref, hist_hbm, cot_hbm, gain_in_hbm, gain_attn_hbm, w_in_ref, w_out_ref,
    out_ref, grad_ref, gains_ref, *rest,
):
    ns = len(STREAMS)
    results, rest = rest[:ns], rest[ns:]
    stream_bufs, rest = rest[: 5 * ns], rest[5 * ns :]
    (
        hist, gains, cots, normed, normed_t, xhat_own, w_own, wo_own, hid, slope, q_heads, k_heads, v_heads, d_heads,
        weights, turn, attended, dpre, stat_own, stat_other, proj, proj_in, dnorm, dnorm_in, gx0, gx1, gx2, gx3,
        lsem, ssem, rsem, psem, qsem, gssem, grsem, fssem, frsem,
    ) = rest
    place = Place()
    core = place.core
    away = 1 - core
    partner = place.partner()

    with jax.named_scope("start"):
        first = pl.multiple_of(core * HALF, HALF)
        loads = [
            pltpu.make_async_copy(hist_hbm, hist, lsem.at[0]),
            pltpu.make_async_copy(gain_in_hbm, gains.at[0], lsem.at[1]),
            pltpu.make_async_copy(cot_hbm, cots.at[core], lsem.at[2]),
        ]
        w_loads = [None] * 4
        for i, g in enumerate((2, 3, 1, 0)):
            columns = pl.ds(pl.multiple_of(g * D + first, HALF), HALF)
            w_loads[g] = pltpu.make_async_copy(w_in_ref.at[:, columns], w_own.at[g], lsem.at[3 + i])
            loads.append(w_loads[g])
        wo_load = pltpu.make_async_copy(w_out_ref.at[pl.ds(first, HALF), :], wo_own, lsem.at[7])
        ga_load = pltpu.make_async_copy(gain_attn_hbm, gains.at[1], lsem.at[8])
        loads += [wo_load, ga_load]
        for load in loads:
            load.start()

        barrier = pltpu.get_barrier_semaphore()
        pl.semaphore_signal(barrier, inc=1, device_id=partner, device_id_type=MESH)
        for axis, n in enumerate(SIZES):
            for d in range(1, n):
                pl.semaphore_signal(
                    barrier,
                    inc=1,
                    device_id=place.device(axis, lax.rem(place.pos[axis] + d, n)),
                    device_id_type=MESH,
                )

    streams = [
        Stream(place, order, stream_bufs[5 * i : 5 * i + 5], results[i].at[core], ssem, rsem, LEVELS * i)
        for i, (order, _) in enumerate(STREAMS)
    ]

    def to_partner(src, dst, i):
        copy = pltpu.make_async_remote_copy(
            src_ref=src,
            dst_ref=dst,
            send_sem=psem.at[i],
            recv_sem=qsem.at[i],
            device_id=partner,
            device_id_type=MESH,
        )
        copy.start()
        return copy

    length = len_ref[0]
    lane_head = lax.broadcasted_iota(jnp.int32, (1, HALF), 1) // DH

    def valid_rows(block):
        row = lax.broadcasted_iota(jnp.int32, (BLK, 1), 0) + block * BLK
        return (row < length).astype(F32)

    def put_heads(ref, block, t):
        for h in range(HEADS):
            ref[block, h * BLK : h * BLK + BLK, :] = jnp.where(lane_head == h, t, jnp.zeros_like(t))

    def heads_beside(t):
        return jnp.concatenate([t[h * BLK : h * BLK + BLK] for h in range(HEADS)], axis=1)

    def project(block, wait):
        for g in (2, 3, 1, 0):
            if wait:
                w_loads[g].wait()
            half = 0.5 * rows_dot(normed[block], w_own[g])
            t = jnp.tanh(half)
            u = half * t
            hidden = (half + u).astype(BF16)
            slope[g, block] = (0.03125 if g == 2 else 0.5) * ((1.0 + t) * (1.0 + half - u))
            if g == 2:
                put_heads(q_heads, block, hidden * (0.5 * SCORE_SCALE))
            else:
                hid[g, block] = hidden
                if g == 3:
                    put_heads(k_heads, block, hidden)
                if g == 1:
                    put_heads(v_heads, block, hidden)

    def attend(tile, q_block, k_block, diagonal):
        half = cols_dot(q_heads[q_block], hid[3, k_block])
        t = jnp.tanh(half)
        u = half * t
        weight = half + u
        turned = (1.0 + t) * (1.0 + half - u)
        if diagonal:
            q_pos = lax.broadcasted_iota(jnp.int32, (HEADS * BLK, BLK), 0) & (BLK - 1)
            k_pos = lax.broadcasted_iota(jnp.int32, (HEADS * BLK, BLK), 1)
            allowed = k_pos <= q_pos
            weight = jnp.where(allowed, weight, 0.0)
            turned = jnp.where(allowed, turned, 0.0)
        weight = weight.astype(BF16)
        weights[tile] = weight
        turn[tile] = turned
        return rows_dot(heads_beside(weight), v_heads[k_block])

    with jax.named_scope("own_project"):
        loads[0].wait()
        loads[1].wait()
        xhat, rstd_in = standardize(hist[...].astype(F32))
        xhat_own[...] = xhat
        normed[core] = (xhat * gains[0]).astype(BF16)
        project(core, True)
    with jax.named_scope("barrier"):
        loads[2].wait()
        pl.semaphore_wait(barrier, 18)
        normed_copy = to_partner(normed.at[core], normed.at[core], 0)
        cots_copy = to_partner(cots.at[core], cots.at[core], 1)
    with jax.named_scope("own_attend"):
        attended[core] = attend(core, core, core, True)
    with jax.named_scope("share_wait"):
        normed_copy.wait_recv()
    with jax.named_scope("other_project"):
        project(away, False)
    with jax.named_scope("other_attend"):
        attended[away] = attend(away, away, away, True)
        attended[1] = attended[1] + attend(2, 1, 0, False)
    with jax.named_scope("d_mixed"):
        cots_copy.wait_recv()
        wo_load.wait()
        ga_load.wait()
        valid = jnp.concatenate([valid_rows(0), valid_rows(1)], axis=0)
        d_proj = (cots[...].reshape(SEQ, D).astype(F32) * valid).astype(BF16)
        gain_attn = gains[1, :, pl.ds(first, HALF)]
        att = attended[...].reshape(SEQ, HALF) * valid
        gating = hid[0].reshape(SEQ, HALF).astype(F32)
        d_mixed = cols_dot(d_proj, wo_own[...])
        g = d_mixed * gain_attn * gating
    with jax.named_scope("stats"):
        half_mean = jnp.mean(att, axis=-1, keepdims=True)
        centered = att - half_mean
        half_sq = jnp.sum(centered * centered, axis=-1, keepdims=True)
        half_g = jnp.sum(g, axis=-1, keepdims=True)
        half_gc = jnp.sum(g * centered, axis=-1, keepdims=True)
        lane = lax.broadcasted_iota(jnp.int32, (SEQ, 128), 1)
        stat_own[...] = jnp.where(
            lane == 0, half_mean, jnp.where(lane == 1, half_sq, jnp.where(lane == 2, half_g, half_gc))
        )
        stat_copy = to_partner(stat_own, stat_other, 2)
        normed_t[...] = normed[...].reshape(SEQ, D).T
    with jax.named_scope("stats_wait"):
        stat_copy.wait_recv()
    with jax.named_scope("norm"):
        other = stat_other[...]
        o_mean, o_sq, o_g, o_gc = (other[:, i : i + 1] for i in range(4))
        mean = 0.5 * (half_mean + o_mean)
        up, o_up = half_mean - mean, o_mean - mean
        var = (half_sq + o_sq + HALF * (up * up + o_up * o_up)) * (1.0 / D)
        rstd = lax.rsqrt(var + EPS)
        mean_g = (half_g + o_g) * (1.0 / D)
        mean_gn = rstd * (half_gc + o_gc + half_g * up + o_g * o_up) * (1.0 / D)
        norm = (att - mean) * rstd
        ng = norm * gain_attn
        mixed = (ng * gating).astype(BF16)
        d_att = (rstd * (g - mean_g - norm * mean_gn) * valid).astype(BF16)
        g_attn = jnp.sum(d_mixed * norm * gating, axis=0, keepdims=True)

    def put(stream, first_row, rows, part):
        n = streams[stream].n
        streams[stream].src[:, :, first_row : first_row + rows, :] = part.astype(BF16).reshape(n[0], n[1], rows, 128)

    def weight_grad(g, d_hidden):
        d_pre = (d_hidden * slope[g].reshape(SEQ, HALF)).astype(BF16)
        dpre[g] = d_pre
        return rows_dot(normed_t[...], d_pre)

    with jax.named_scope("grads_u"):
        g_u = weight_grad(0, d_mixed * ng)
        g_out = rows_dot(mixed.T, d_proj)
        for half in range(2):
            put(half, 0, 16, g_u[:, half * 128 : half * 128 + 128])
            blocks = [g_out[:, (2 * half + i) * 128 : (2 * half + i) * 128 + 128] for i in range(2)]
            put(half, 16, 16, jnp.concatenate(blocks, axis=0))
            streams[half].scatter1()
    with jax.named_scope("grads_v"):
        for block in range(2):
            put_heads(d_heads, block, d_att[block * BLK : block * BLK + BLK])
        d_values_0 = sum_rows_dot(weights[0], d_heads[0]) + sum_rows_dot(weights[2], d_heads[1])
        d_values_1 = sum_rows_dot(weights[1], d_heads[1])
        g_v = weight_grad(1, jnp.concatenate([d_values_0, d_values_1], axis=0))
        for half in range(2):
            put(2 + half, 0, 16, g_v[:, half * 128 : half * 128 + 128])
            streams[2 + half].scatter1()
    with jax.named_scope("grads_k"):
        slopes = []
        for tile, (q_block, k_block) in enumerate(((0, 0), (1, 1), (1, 0))):
            slopes.append((cols_dot(d_heads[q_block], hid[1, k_block]) * turn[tile]).astype(BF16))
        d_keys_0 = sum_rows_dot(slopes[0], q_heads[0]) + sum_rows_dot(slopes[2], q_heads[1])
        d_keys_1 = sum_rows_dot(slopes[1], q_heads[1])
        g_k = weight_grad(3, jnp.concatenate([d_keys_0, d_keys_1], axis=0))
        for half in range(2):
            put(6 + half, 0, 16, g_k[:, half * 128 : half * 128 + 128])
            streams[6 + half].scatter1()
    with jax.named_scope("grads_q"):
        d_query_0 = rows_dot(heads_beside(slopes[0]), k_heads[0])
        d_query_1 = rows_dot(heads_beside(slopes[1]), k_heads[1]) + rows_dot(heads_beside(slopes[2]), k_heads[0])
        g_q = weight_grad(2, jnp.concatenate([d_query_0, d_query_1], axis=0))
        for half in range(2):
            put(4 + half, 0, 16, g_q[:, half * 128 : half * 128 + 128])
            streams[4 + half].scatter1()
    with jax.named_scope("scatter2_u"):
        for s in streams[:2]:
            s.scatter2()
    with jax.named_scope("d_norm"):
        d_norm = cols_dot(dpre[0], w_own[0])
        for g in range(1, 4):
            d_norm = d_norm + cols_dot(dpre[g], w_own[g])
        dnorm[...] = d_norm.reshape(2, BLK, D)
        dnorm_copy = to_partner(dnorm.at[away], dnorm_in, 3)
    with jax.named_scope("scatter2_v"):
        for s in streams[2:4]:
            s.scatter2()
    with jax.named_scope("proj"):
        proj[...] = rows_dot(mixed, wo_own[...]).reshape(2, BLK, D)
        proj_copy = to_partner(proj.at[away], proj_in, 4)

    with jax.named_scope("gain_sums"):
        xhat = xhat_own[...]
        dnorm_copy.wait_recv()
        d_norm = dnorm[core] + dnorm_in[...]
        gain_part = jnp.sum(d_norm * xhat, axis=0, keepdims=True)
        mine = (core == 0).astype(F32)
        gx0_own = gx0.at[core]
        for i in range(4):
            gx0_own[i : i + 1, :] = gain_part[:, i * 128 : i * 128 + 128]
        for i in range(2):
            part = g_attn[:, i * 128 : i * 128 + 128]
            gx0_own[4 + i : 5 + i, :] = part * mine
            gx0_own[6 + i : 7 + i, :] = part * (1.0 - mine)
        gain_copy = to_partner(gx0_own, gx0_own, 5)

    def gains_fan(axis, buf):
        n, me = SIZES[axis], place.pos[axis]
        own = buf.at[me]
        for d in range(1, n):
            pltpu.make_async_remote_copy(
                src_ref=own,
                dst_ref=own,
                send_sem=gssem.at[axis],
                recv_sem=grsem.at[axis],
                device_id=place.device(axis, lax.rem(me + d, n)),
                device_id_type=MESH,
            ).start()

    def gains_total(axis, buf):
        n = SIZES[axis]
        wait_bytes(buf.at[pl.ds(0, n - 1)], grsem.at[axis])
        acc = buf[0]
        for j in range(1, n):
            acc = acc + buf[j]
        return acc

    with jax.named_scope("scatter2_k"):
        for s in streams[6:]:
            s.scatter2()
    with jax.named_scope("scatter2_q"):
        for s in streams[4:6]:
            s.scatter2()
    with jax.named_scope("gains_x"):
        gain_copy.wait_recv()
        gx1[place.pos[0]] = gx0[0] + gx0[1]
        gains_fan(0, gx1)

    with jax.named_scope("grad_history"):
        e = d_norm * gains[0]
        d_hist = rstd_in * (
            e - jnp.mean(e, axis=-1, keepdims=True) - xhat * jnp.mean(e * xhat, axis=-1, keepdims=True)
        )
        grad_ref[...] = (cots[core].astype(F32) + d_hist).astype(BF16)
        proj_copy.wait_recv()
        out_ref[...] = (hist[...].astype(F32) + valid_rows(core) * (proj[core] + proj_in[...])).astype(BF16)

    with jax.named_scope("exchange_uv"):
        for s in streams[:4]:
            s.exchange()
    with jax.named_scope("gains_y"):
        gx2[place.pos[1]] = gains_total(0, gx1)
        gains_fan(1, gx2)
    with jax.named_scope("exchange_qk"):
        for s in streams[4:]:
            s.exchange()
    with jax.named_scope("gather2_uv"):
        for s in streams[:4]:
            s.gather2()
    with jax.named_scope("gains_z"):
        gx3[place.pos[2]] = gains_total(1, gx2)
        gains_fan(2, gx3)
    with jax.named_scope("gather2_qk"):
        for s in streams[4:]:
            s.gather2()
    with jax.named_scope("gather1_uv"):
        for s in streams[:4]:
            s.gather1()
    with jax.named_scope("gather1_qk"):
        for s in streams[4:]:
            s.gather1()
    with jax.named_scope("gains_end"):
        gains_ref[...] = gains_total(2, gx3)
    with jax.named_scope("finish"):
        forwards = []
        for i, s in enumerate(streams):
            s.finish()
            forwards.append(
                pltpu.make_async_remote_copy(
                    src_ref=s.res,
                    dst_ref=s.res,
                    send_sem=fssem.at[i],
                    recv_sem=frsem.at[i],
                    device_id=partner,
                    device_id_type=MESH,
                )
            )
            forwards[-1].start()
    with jax.named_scope("drain"):
        for axis, buf in enumerate((gx1, gx2, gx3)):
            wait_bytes(buf.at[pl.ds(0, SIZES[axis] - 1)], gssem.at[axis])
        for copy in (normed_copy, cots_copy, stat_copy, dnorm_copy, proj_copy, gain_copy):
            copy.wait_send()
        for s in streams:
            s.drain()
        for copy in forwards:
            copy.wait()


def widen_kernel(factor, *refs):
    ns = len(STREAMS)
    out_in, grad_in, gains_ref, results = refs[0], refs[1], refs[2], refs[3 : 3 + ns]
    out_ref, grad_ref, w_in_ref, w_out_ref, gin_ref, gattn_ref, w_in_wide, w_out_wide, gains_wide, sem = refs[3 + ns :]
    copies = []

    def send(src, dst):
        copies.append(pltpu.make_async_copy(src, dst, sem.at[len(copies)]))
        copies[-1].start()

    def wide(t):
        return t.astype(F32) * factor

    for half in range(2):
        for core in range(2):
            part = wide(results[half][core, :, :, 16:32, :].reshape(D, 128))
            for i in range(2):
                column = (2 * half + i) * 128
                w_out_wide[core * HALF : core * HALF + HALF, column : column + 128] = part[i * HALF : i * HALF + HALF]
    send(w_out_wide, w_out_ref)
    for g in range(4):
        for core in range(2):
            for half in range(2):
                column = (4 * g + 2 * core + half) * 128
                part = results[2 * g + half][core, :, :, 0:16, :].reshape(D, 128)
                w_in_wide[:, column : column + 128] = wide(part)
            columns = slice((4 * g + 2 * core) * 128, (4 * g + 2 * core + 2) * 128)
            send(w_in_wide.at[:, columns], w_in_ref.at[:, columns])
    for i in range(4):
        gains_wide[0, :, i * 128 : i * 128 + 128] = gains_ref[i : i + 1, :] * factor
        gains_wide[1, :, i * 128 : i * 128 + 128] = gains_ref[4 + i : 5 + i, :] * factor
    send(gains_wide.at[0], gin_ref)
    send(gains_wide.at[1], gattn_ref)
    send(out_in, out_ref)
    send(grad_in, grad_ref)
    for copy in copies:
        copy.wait()


VMEM = pl.BlockSpec(memory_space=pltpu.VMEM)
SMEM = pl.BlockSpec(memory_space=pltpu.SMEM)
HBM = pl.BlockSpec(memory_space=pltpu.HBM)


def shape(dims, kind):
    return jax.ShapeDtypeStruct(dims, kind)


def per_device(users, history, lengths, input_gain, gain_attn, w_in, w_out, cotangent):
    history, cotangent = history[0], cotangent[0]
    input_gain, gain_attn = input_gain[None], gain_attn[None]
    operands = [history, cotangent, input_gain, gain_attn, w_in, w_out]
    operands = [pltpu.with_memory_space_constraint(t, pltpu.HBM) for t in operands]
    dma = pltpu.SemaphoreType.DMA

    buffers, result_shapes = [], []
    for order, rows in STREAMS:
        n = [SIZES[a] for a in order]
        result_shapes.append(shape((2, n[0], n[1], rows, 128), BF16))
        buffers += [
            pltpu.VMEM((n[0], n[1], rows, 128), BF16),
            pltpu.VMEM((n[0], n[1], rows, 128), BF16),
            pltpu.VMEM((n[1], rows, 128), BF16),
            pltpu.VMEM((n[1], rows, 128), BF16),
            pltpu.VMEM((n[2], rows, 128), BF16),
        ]
    ns = len(STREAMS)
    heads = pltpu.VMEM((2, HEADS * BLK, HALF), BF16)
    out, grad, gains, *results = pl.pallas_call(
        layer_kernel,
        out_shape=(shape((BLK, D), BF16), shape((BLK, D), BF16), shape((8, 128), F32), *result_shapes),
        in_specs=[SMEM] + [HBM] * 6,
        out_specs=(VMEM,) * (3 + ns),
        scratch_shapes=buffers
        + [
            pltpu.VMEM((BLK, D), BF16),
            pltpu.VMEM((2, 1, D), F32),
            pltpu.VMEM((2, BLK, D), BF16),
            pltpu.VMEM((2, BLK, D), BF16),
            pltpu.VMEM((D, SEQ), BF16),
            pltpu.VMEM((BLK, D), F32),
            pltpu.VMEM((4, D, HALF), BF16),
            pltpu.VMEM((HALF, D), BF16),
            pltpu.VMEM((4, 2, BLK, HALF), BF16),
            pltpu.VMEM((4, 2, BLK, HALF), F32),
            heads,
            heads,
            heads,
            heads,
            pltpu.VMEM((3, HEADS * BLK, BLK), BF16),
            pltpu.VMEM((3, HEADS * BLK, BLK), F32),
            pltpu.VMEM((2, BLK, HALF), F32),
            pltpu.VMEM((4, SEQ, HALF), BF16),
            pltpu.VMEM((SEQ, 128), F32),
            pltpu.VMEM((SEQ, 128), F32),
            pltpu.VMEM((2, BLK, D), F32),
            pltpu.VMEM((BLK, D), F32),
            pltpu.VMEM((2, BLK, D), F32),
            pltpu.VMEM((BLK, D), F32),
            pltpu.VMEM((2, 8, 128), F32),
            pltpu.VMEM((4, 8, 128), F32),
            pltpu.VMEM((8, 8, 128), F32),
            pltpu.VMEM((8, 8, 128), F32),
            dma((9,)),
            dma((LEVELS * ns,)),
            dma((LEVELS * ns,)),
            dma((6,)),
            dma((6,)),
            dma((3,)),
            dma((3,)),
            dma((ns,)),
            dma((ns,)),
        ],
        compiler_params=pltpu.CompilerParams(collective_id=1, has_side_effects=True, vmem_limit_bytes=48 << 20),
        name="layer",
    )(lengths, *operands)

    factor = 1.0 / math.sqrt(users * SEQ)
    out, grad, g_in, g_out, gain_in_grad, gain_attn_grad = pl.pallas_call(
        functools.partial(widen_kernel, factor),
        out_shape=(
            shape((BLK, D), BF16),
            shape((BLK, D), BF16),
            shape((D, 4 * D), F32),
            shape((D, D), F32),
            shape((1, D), F32),
            shape((1, D), F32),
        ),
        in_specs=[VMEM] * (3 + ns),
        out_specs=(HBM,) * 6,
        scratch_shapes=[
            pltpu.VMEM((D, 4 * D), F32),
            pltpu.VMEM((D, D), F32),
            pltpu.VMEM((2, 1, D), F32),
            dma((13,)),
        ],
        compiler_params=pltpu.CompilerParams(vmem_limit_bytes=32 << 20),
        name="widen",
    )(out, grad, gains, *results)
    return out[None], grad[None], g_in, g_out, gain_in_grad[0], gain_attn_grad[0]


def solution(mesh):
    placed = (P("dp", "ctx", None), P("dp"), P(), P(), P(), P(), P("dp", "ctx", None))
    return jax.shard_map(
        functools.partial(per_device, mesh.shape["dp"]),
        mesh=mesh,
        in_specs=placed,
        out_specs=(P("dp", "ctx", None), P("dp", "ctx", None), P(), P(), P(), P()),
        check_vma=False,
    )
```

```python
import functools
import math

import jax
import jax.numpy as jnp
from jax import lax
from jax.experimental import pallas as pl
from jax.experimental.pallas import tpu as pltpu
from jax.sharding import PartitionSpec as P

MESH = pl.DeviceIdType.MESH
F32 = jnp.float32
BF16 = jnp.bfloat16
D = 512
DH = 64
BLK = 128
SEQ = 256
HALF = 256
HEADS = 4
SIZES = (4, 8, 8)
EPS = 1e-05
SCORE_SCALE = 1.0 / math.sqrt(DH)
XYZ, XZY, YXZ, ZXY = (0, 1, 2), (0, 2, 1), (1, 0, 2), (2, 0, 1)
ROWS = 16
STREAMS = (XYZ, XZY, YXZ, ZXY, YXZ, ZXY, XYZ, XZY, XYZ, XZY)
GATING, OUT, VALUES, KEYS, QUERIES = 0, 2, 4, 6, 8
STREAM_OF = (GATING, VALUES, QUERIES, KEYS)
LEVELS = 5


def dot(left, right, dims):
    return lax.dot_general(left, right, (dims, ((), ())), preferred_element_type=F32)


def rows_dot(left, right):
    return dot(left, right, ((1,), (0,)))


def cols_dot(left, right):
    return dot(left, right, ((1,), (1,)))


def sum_rows_dot(left, right):
    return dot(left, right, ((0,), (0,)))


def sigmoid(t):
    return 0.5 * jnp.tanh(0.5 * t) + 0.5


def standardize(t):
    centered = t - jnp.mean(t, axis=-1, keepdims=True)
    rstd = lax.rsqrt(jnp.mean(centered * centered, axis=-1, keepdims=True) + EPS)
    return centered * rstd, rstd


class Place:
    def __init__(self):
        self.dp = lax.axis_index("dp")
        self.core = lax.axis_index("ctx")
        self.pos = (lax.rem(self.dp, 4), lax.rem(self.dp // 4, 8), self.dp // 32)
        self.partner = (self.dp, 1 - self.core)
        self.peers = []
        for axis, (n, stride) in enumerate(zip(SIZES, (1, 4, 32))):
            me = self.pos[axis]
            others = [lax.rem(me + d, n) for d in sorted(range(1, n), key=lambda d: -min(d, n - d))]
            self.peers.append([(k, (self.dp + (k - me) * stride, self.core)) for k in others])


def wait_bytes(region, sem):
    pltpu.make_async_copy(region, region, sem).wait()


class Stream:
    def __init__(self, place, order, bufs, result, ssem, rsem, base):
        self.place, self.order, self.base = place, order, base
        self.src, self.r1, self.s1, self.r2, self.r3 = bufs
        self.res = result
        self.ssem, self.rsem = ssem, rsem
        self.n = [SIZES[a] for a in order]
        self.me = [place.pos[a] for a in order]

    def fan(self, phase, level, src, dst):
        for k, device in self.place.peers[self.order[level]]:
            pltpu.make_async_remote_copy(
                src_ref=src(k),
                dst_ref=dst,
                send_sem=self.ssem.at[self.base + phase],
                recv_sem=self.rsem.at[self.base + phase],
                device_id=device,
                device_id_type=MESH,
            ).start()

    def wait_recv(self, phase, region):
        wait_bytes(region, self.rsem.at[self.base + phase])

    def total(self, ref, n):
        acc = ref[0].astype(F32)
        for j in range(1, n):
            acc = acc + ref[j].astype(F32)
        return acc.astype(BF16)

    def scatter1(self):
        self.fan(0, 0, lambda k: self.src.at[k], self.r1.at[self.me[0]])

    def scatter2(self):
        n, me = self.n[0], self.me[0]
        self.wait_recv(0, self.r1.at[pl.ds(0, n - 1)])
        self.r1[me] = self.src[me]
        self.s1[...] = self.total(self.r1, n)
        self.fan(1, 1, lambda k: self.s1.at[k], self.r2.at[self.me[1]])

    def exchange(self):
        n, me = self.n[1], self.me[1]
        self.wait_recv(1, self.r2.at[pl.ds(0, n - 1)])
        self.r2[me] = self.s1[me]
        own = self.r3.at[self.me[2]]
        own[...] = self.total(self.r2, n)
        self.fan(2, 2, lambda k: own, own)

    def gather2(self):
        n = self.n[2]
        self.wait_recv(2, self.r3.at[pl.ds(0, n - 1)])
        own = self.res.at[self.me[0], self.me[1]]
        own[...] = self.total(self.r3, n)
        self.fan(3, 1, lambda k: own, own)

    def gather1(self):
        own = self.res.at[self.me[0]]
        self.wait_recv(3, own.at[pl.ds(0, self.n[1] - 1)])
        self.fan(4, 0, lambda k: own, own)

    def finish(self):
        self.wait_recv(4, self.res.at[pl.ds(0, self.n[0] - 1)])

    def drain(self):
        n = self.n
        regions = (
            self.r1.at[pl.ds(0, n[0] - 1)],
            self.r2.at[pl.ds(0, n[1] - 1)],
            self.r3.at[pl.ds(0, n[2] - 1)],
            self.res.at[0, pl.ds(0, n[1] - 1)],
            self.res.at[pl.ds(0, n[0] - 1)],
        )
        for phase, region in enumerate(regions):
            wait_bytes(region, self.ssem.at[self.base + phase])


def layer_kernel(
    len_ref, hist_hbm, cot_hbm, gain_in_hbm, gain_attn_hbm, w_in_ref, w_out_ref,
    out_ref, grad_ref, gains_ref, *rest,
):
    ns = len(STREAMS)
    results, rest = rest[:ns], rest[ns:]
    stream_bufs, rest = rest[: 5 * ns], rest[5 * ns :]
    (
        hist, gains, cots, normed, normed_t, xhat_own, w_own, wo_own, hid, slope, q_heads, k_heads, v_heads, d_heads,
        weights, turn, attended, dpre, stat_own, stat_other, proj, proj_in, dnorm, dnorm_in, gx0, gx1, gx2, gx3,
        lsem, ssem, rsem, psem, qsem, gssem, grsem, fssem, frsem,
    ) = rest
    place = Place()
    core = place.core
    away = 1 - core
    partner = place.partner

    with jax.named_scope("start"):
        first = pl.multiple_of(core * HALF, HALF)
        loads = [
            pltpu.make_async_copy(hist_hbm, hist, lsem.at[0]),
            pltpu.make_async_copy(gain_in_hbm, gains.at[0], lsem.at[1]),
            pltpu.make_async_copy(cot_hbm, cots.at[core], lsem.at[2]),
        ]
        w_loads = [None] * 4
        for i, g in enumerate((2, 3, 1, 0)):
            columns = pl.ds(pl.multiple_of(g * D + first, HALF), HALF)
            w_loads[g] = pltpu.make_async_copy(w_in_ref.at[:, columns], w_own.at[g], lsem.at[3 + i])
            loads.append(w_loads[g])
        wo_load = pltpu.make_async_copy(w_out_ref.at[pl.ds(first, HALF), :], wo_own, lsem.at[7])
        ga_load = pltpu.make_async_copy(gain_attn_hbm, gains.at[1], lsem.at[8])
        loads += [wo_load, ga_load]
        for load in loads:
            load.start()

        barrier = pltpu.get_barrier_semaphore()
        pl.semaphore_signal(barrier, inc=1, device_id=partner, device_id_type=MESH)
        for peers in place.peers:
            for _, device in peers:
                pl.semaphore_signal(barrier, inc=1, device_id=device, device_id_type=MESH)

    streams = [
        Stream(place, order, stream_bufs[5 * i : 5 * i + 5], results[i].at[core], ssem, rsem, LEVELS * i)
        for i, order in enumerate(STREAMS)
    ]

    def to_partner(src, dst, i):
        copy = pltpu.make_async_remote_copy(
            src_ref=src,
            dst_ref=dst,
            send_sem=psem.at[i],
            recv_sem=qsem.at[i],
            device_id=partner,
            device_id_type=MESH,
        )
        copy.start()
        return copy

    lane_head = lax.broadcasted_iota(jnp.int32, (1, HALF), 1) // DH

    def valid_rows(block):
        row = lax.broadcasted_iota(jnp.int32, (BLK, 1), 0) + block * BLK
        return (row < len_ref[0]).astype(F32)

    def put_heads(ref, block, t):
        for h in range(HEADS):
            ref[block, h * BLK : h * BLK + BLK, :] = jnp.where(lane_head == h, t, jnp.zeros_like(t))

    def heads_beside(t):
        return jnp.concatenate([t[h * BLK : h * BLK + BLK] for h in range(HEADS)], axis=1)

    def project(block, wait):
        for g in (2, 3, 1, 0):
            if wait:
                w_loads[g].wait()
            half = 0.5 * rows_dot(normed[block], w_own[g])
            t = jnp.tanh(half)
            u = half * t
            hidden = (half + u).astype(BF16)
            slope[g, block] = (0.03125 if g == 2 else 0.5) * ((1.0 + t) * (1.0 + half - u))
            if g == 2:
                put_heads(q_heads, block, hidden * (0.5 * SCORE_SCALE))
            else:
                hid[g, block] = hidden
                if g == 3:
                    put_heads(k_heads, block, hidden)
                if g == 1:
                    put_heads(v_heads, block, hidden)

    def attend(tile, q_block, k_block, diagonal):
        half = cols_dot(q_heads[q_block], hid[3, k_block])
        t = jnp.tanh(half)
        u = half * t
        weight = half + u
        turned = (1.0 + t) * (1.0 + half - u)
        if diagonal:
            q_pos = lax.broadcasted_iota(jnp.int32, (HEADS * BLK, BLK), 0) & (BLK - 1)
            k_pos = lax.broadcasted_iota(jnp.int32, (HEADS * BLK, BLK), 1)
            allowed = k_pos <= q_pos
            weight = jnp.where(allowed, weight, 0.0)
            turned = jnp.where(allowed, turned, 0.0)
        weight = weight.astype(BF16)
        weights[tile] = weight
        turn[tile] = turned
        return rows_dot(heads_beside(weight), v_heads[k_block])

    with jax.named_scope("own_project"):
        loads[0].wait()
        loads[1].wait()
        xhat, rstd_in = standardize(hist[...].astype(F32))
        xhat_own[...] = xhat
        normed[core] = (xhat * gains[0]).astype(BF16)
        project(core, True)
    with jax.named_scope("barrier"):
        loads[2].wait()
        pl.semaphore_wait(barrier, 18)
        normed_copy = to_partner(normed.at[core], normed.at[core], 0)
        cots_copy = to_partner(cots.at[core], cots.at[core], 1)
    with jax.named_scope("own_attend"):
        attended[core] = attend(core, core, core, True)
    with jax.named_scope("share_wait"):
        normed_copy.wait_recv()
    with jax.named_scope("other_project"):
        project(away, False)
    with jax.named_scope("other_attend"):
        attended[away] = attend(away, away, away, True)
        attended[1] = attended[1] + attend(2, 1, 0, False)
    with jax.named_scope("d_mixed"):
        cots_copy.wait_recv()
        wo_load.wait()
        ga_load.wait()
        valid = jnp.concatenate([valid_rows(0), valid_rows(1)], axis=0)
        d_proj = (cots[...].reshape(SEQ, D).astype(F32) * valid).astype(BF16)
        gain_attn = gains[1, :, pl.ds(first, HALF)]
        att = attended[...].reshape(SEQ, HALF) * valid
        gating = hid[0].reshape(SEQ, HALF).astype(F32)
        d_mixed = cols_dot(d_proj, wo_own[...])
        g = d_mixed * gain_attn * gating
    with jax.named_scope("stats"):
        half_mean = jnp.mean(att, axis=-1, keepdims=True)
        centered = att - half_mean
        half_sq = jnp.sum(centered * centered, axis=-1, keepdims=True)
        half_g = jnp.sum(g, axis=-1, keepdims=True)
        half_gc = jnp.sum(g * centered, axis=-1, keepdims=True)
        lane = lax.broadcasted_iota(jnp.int32, (SEQ, 128), 1)
        stat_own[...] = jnp.where(
            lane == 0, half_mean, jnp.where(lane == 1, half_sq, jnp.where(lane == 2, half_g, half_gc))
        )
        stat_copy = to_partner(stat_own, stat_other, 2)
        normed_t[...] = normed[...].reshape(SEQ, D).T
    with jax.named_scope("stats_wait"):
        stat_copy.wait_recv()
    with jax.named_scope("norm"):
        other = stat_other[...]
        o_mean, o_sq, o_g, o_gc = (other[:, i : i + 1] for i in range(4))
        mean = 0.5 * (half_mean + o_mean)
        up, o_up = half_mean - mean, o_mean - mean
        var = (half_sq + o_sq + HALF * (up * up + o_up * o_up)) * (1.0 / D)
        rstd = lax.rsqrt(var + EPS)
        mean_g = (half_g + o_g) * (1.0 / D)
        mean_gn = rstd * (half_gc + o_gc + half_g * up + o_g * o_up) * (1.0 / D)
        norm = (att - mean) * rstd
        ng = norm * gain_attn
        mixed = (ng * gating).astype(BF16)
        d_att = (rstd * (g - mean_g - norm * mean_gn) * valid).astype(BF16)
        g_attn = jnp.sum(d_mixed * norm * gating, axis=0, keepdims=True)

    def put(group, halves):
        for half, part in enumerate(halves):
            stream = streams[group + half]
            stream.src[...] = part.astype(BF16).reshape(stream.n[0], stream.n[1], ROWS, 128)
            stream.scatter1()

    def columns_in_halves(t):
        return [t[:, :128], t[:, 128:]]

    def of(group):
        return streams[group : group + 2]

    def weight_grad(g, d_hidden):
        d_pre = (d_hidden * slope[g].reshape(SEQ, HALF)).astype(BF16)
        dpre[g] = d_pre
        return rows_dot(normed_t[...], d_pre)

    with jax.named_scope("grads_u"):
        put(GATING, columns_in_halves(weight_grad(0, d_mixed * ng)))
        g_out = rows_dot(mixed.T, d_proj)
        g_out = [g_out[:, i * 128 : i * 128 + 128] for i in range(4)]
        put(OUT, [jnp.concatenate(g_out[:2], axis=0), jnp.concatenate(g_out[2:], axis=0)])
    with jax.named_scope("grads_v"):
        for block in range(2):
            put_heads(d_heads, block, d_att[block * BLK : block * BLK + BLK])
        d_values_0 = sum_rows_dot(weights[0], d_heads[0]) + sum_rows_dot(weights[2], d_heads[1])
        d_values_1 = sum_rows_dot(weights[1], d_heads[1])
        put(VALUES, columns_in_halves(weight_grad(1, jnp.concatenate([d_values_0, d_values_1], axis=0))))
    with jax.named_scope("grads_k"):
        slopes = []
        for tile, (q_block, k_block) in enumerate(((0, 0), (1, 1), (1, 0))):
            slopes.append((cols_dot(d_heads[q_block], hid[1, k_block]) * turn[tile]).astype(BF16))
        d_keys_0 = sum_rows_dot(slopes[0], q_heads[0]) + sum_rows_dot(slopes[2], q_heads[1])
        d_keys_1 = sum_rows_dot(slopes[1], q_heads[1])
        put(KEYS, columns_in_halves(weight_grad(3, jnp.concatenate([d_keys_0, d_keys_1], axis=0))))
    with jax.named_scope("grads_q"):
        d_query_0 = rows_dot(heads_beside(slopes[0]), k_heads[0])
        d_query_1 = rows_dot(heads_beside(slopes[1]), k_heads[1]) + rows_dot(heads_beside(slopes[2]), k_heads[0])
        put(QUERIES, columns_in_halves(weight_grad(2, jnp.concatenate([d_query_0, d_query_1], axis=0))))
    with jax.named_scope("scatter2_u"):
        for s in of(GATING):
            s.scatter2()
    with jax.named_scope("d_norm"):
        d_norm = cols_dot(dpre[0], w_own[0])
        for g in range(1, 4):
            d_norm = d_norm + cols_dot(dpre[g], w_own[g])
        dnorm[...] = d_norm.reshape(2, BLK, D)
        dnorm_copy = to_partner(dnorm.at[away], dnorm_in, 3)
    with jax.named_scope("scatter2_out"):
        for s in of(OUT):
            s.scatter2()
    with jax.named_scope("proj"):
        proj[...] = rows_dot(mixed, wo_own[...]).reshape(2, BLK, D)
        proj_copy = to_partner(proj.at[away], proj_in, 4)

    with jax.named_scope("gain_sums"):
        xhat = xhat_own[...]
        dnorm_copy.wait_recv()
        d_norm = dnorm[core] + dnorm_in[...]
        gain_part = jnp.sum(d_norm * xhat, axis=0, keepdims=True)
        mine = (core == 0).astype(F32)
        gx0_own = gx0.at[core]
        for i in range(4):
            gx0_own[i : i + 1, :] = gain_part[:, i * 128 : i * 128 + 128]
        for i in range(2):
            part = g_attn[:, i * 128 : i * 128 + 128]
            gx0_own[4 + i : 5 + i, :] = part * mine
            gx0_own[6 + i : 7 + i, :] = part * (1.0 - mine)
        gain_copy = to_partner(gx0_own, gx0_own, 5)

    def gains_fan(axis, buf):
        own = buf.at[place.pos[axis]]
        for _, device in place.peers[axis]:
            pltpu.make_async_remote_copy(
                src_ref=own,
                dst_ref=own,
                send_sem=gssem.at[axis],
                recv_sem=grsem.at[axis],
                device_id=device,
                device_id_type=MESH,
            ).start()

    def gains_total(axis, buf):
        n = SIZES[axis]
        wait_bytes(buf.at[pl.ds(0, n - 1)], grsem.at[axis])
        acc = buf[0]
        for j in range(1, n):
            acc = acc + buf[j]
        return acc

    with jax.named_scope("scatter2_rest"):
        for s in of(KEYS) + of(QUERIES) + of(VALUES):
            s.scatter2()
    with jax.named_scope("gains_x"):
        gain_copy.wait_recv()
        gx1[place.pos[0]] = gx0[0] + gx0[1]
        gains_fan(0, gx1)

    with jax.named_scope("grad_history"):
        e = d_norm * gains[0]
        d_hist = rstd_in * (
            e - jnp.mean(e, axis=-1, keepdims=True) - xhat * jnp.mean(e * xhat, axis=-1, keepdims=True)
        )
        grad_ref[...] = (cots[core].astype(F32) + d_hist).astype(BF16)
        proj_copy.wait_recv()
        out_ref[...] = (hist[...].astype(F32) + valid_rows(core) * (proj[core] + proj_in[...])).astype(BF16)

    with jax.named_scope("exchange_first"):
        for s in of(GATING) + of(OUT):
            s.exchange()
    with jax.named_scope("gains_y"):
        gx2[place.pos[1]] = gains_total(0, gx1)
        gains_fan(1, gx2)
    with jax.named_scope("exchange_rest"):
        for s in of(KEYS) + of(VALUES) + of(QUERIES):
            s.exchange()
    with jax.named_scope("gather2_first"):
        for s in of(GATING) + of(OUT):
            s.gather2()
    with jax.named_scope("gains_z"):
        gx3[place.pos[2]] = gains_total(1, gx2)
        gains_fan(2, gx3)
    with jax.named_scope("gather2_rest"):
        for s in of(KEYS) + of(VALUES) + of(QUERIES):
            s.gather2()
    order = of(OUT) + of(GATING) + of(VALUES) + of(KEYS) + of(QUERIES)
    with jax.named_scope("gather1"):
        for s in order:
            s.gather1()
    with jax.named_scope("gains_end"):
        gains_ref[...] = gains_total(2, gx3)
    with jax.named_scope("finish"):
        forwards = []
        for i, s in enumerate(order):
            s.finish()
            forwards.append(
                pltpu.make_async_remote_copy(
                    src_ref=s.res,
                    dst_ref=s.res,
                    send_sem=fssem.at[i],
                    recv_sem=frsem.at[i],
                    device_id=partner,
                    device_id_type=MESH,
                )
            )
            forwards[-1].start()
    with jax.named_scope("drain"):
        for axis, buf in enumerate((gx1, gx2, gx3)):
            wait_bytes(buf.at[pl.ds(0, SIZES[axis] - 1)], gssem.at[axis])
        for copy in (normed_copy, cots_copy, stat_copy, dnorm_copy, proj_copy, gain_copy):
            copy.wait_send()
        for s in streams:
            s.drain()
        for copy in forwards:
            copy.wait()


def widen_kernel(factor, *refs):
    ns = len(STREAMS)
    out_in, grad_in, gains_ref, results = refs[0], refs[1], refs[2], refs[3 : 3 + ns]
    out_ref, grad_ref, w_in_ref, w_out_ref, gin_ref, gattn_ref, w_in_wide, w_out_wide, gains_wide, sem = refs[3 + ns :]
    copies = []

    def send(src, dst):
        copies.append(pltpu.make_async_copy(src, dst, sem.at[len(copies)]))
        copies[-1].start()

    def wide(t):
        return t.astype(F32) * factor

    for half in range(2):
        for core in range(2):
            part = wide(results[OUT + half][core].reshape(D, 128))
            for i in range(2):
                column = (2 * half + i) * 128
                w_out_wide[core * HALF : core * HALF + HALF, column : column + 128] = part[i * HALF : i * HALF + HALF]
    send(w_out_wide, w_out_ref)
    for g in range(4):
        for core in range(2):
            for half in range(2):
                column = (4 * g + 2 * core + half) * 128
                part = results[STREAM_OF[g] + half][core].reshape(D, 128)
                w_in_wide[:, column : column + 128] = wide(part)
            columns = slice((4 * g + 2 * core) * 128, (4 * g + 2 * core + 2) * 128)
            send(w_in_wide.at[:, columns], w_in_ref.at[:, columns])
    for i in range(4):
        gains_wide[0, :, i * 128 : i * 128 + 128] = gains_ref[i : i + 1, :] * factor
        gains_wide[1, :, i * 128 : i * 128 + 128] = gains_ref[4 + i : 5 + i, :] * factor
    send(gains_wide.at[0], gin_ref)
    send(gains_wide.at[1], gattn_ref)
    send(out_in, out_ref)
    send(grad_in, grad_ref)
    for copy in copies:
        copy.wait()


VMEM = pl.BlockSpec(memory_space=pltpu.VMEM)
SMEM = pl.BlockSpec(memory_space=pltpu.SMEM)
HBM = pl.BlockSpec(memory_space=pltpu.HBM)


def shape(dims, kind):
    return jax.ShapeDtypeStruct(dims, kind)


def per_device(users, history, lengths, input_gain, gain_attn, w_in, w_out, cotangent):
    history, cotangent = history[0], cotangent[0]
    input_gain, gain_attn = input_gain[None], gain_attn[None]
    operands = [history, cotangent, input_gain, gain_attn, w_in, w_out]
    operands = [pltpu.with_memory_space_constraint(t, pltpu.HBM) for t in operands]
    dma = pltpu.SemaphoreType.DMA

    buffers, result_shapes = [], []
    for order in STREAMS:
        n = [SIZES[a] for a in order]
        result_shapes.append(shape((2, n[0], n[1], ROWS, 128), BF16))
        buffers += [
            pltpu.VMEM((n[0], n[1], ROWS, 128), BF16),
            pltpu.VMEM((n[0], n[1], ROWS, 128), BF16),
            pltpu.VMEM((n[1], ROWS, 128), BF16),
            pltpu.VMEM((n[1], ROWS, 128), BF16),
            pltpu.VMEM((n[2], ROWS, 128), BF16),
        ]
    ns = len(STREAMS)
    heads = pltpu.VMEM((2, HEADS * BLK, HALF), BF16)
    out, grad, gains, *results = pl.pallas_call(
        layer_kernel,
        out_shape=(shape((BLK, D), BF16), shape((BLK, D), BF16), shape((8, 128), F32), *result_shapes),
        in_specs=[SMEM] + [HBM] * 6,
        out_specs=(VMEM,) * (3 + ns),
        scratch_shapes=buffers
        + [
            pltpu.VMEM((BLK, D), BF16),
            pltpu.VMEM((2, 1, D), F32),
            pltpu.VMEM((2, BLK, D), BF16),
            pltpu.VMEM((2, BLK, D), BF16),
            pltpu.VMEM((D, SEQ), BF16),
            pltpu.VMEM((BLK, D), F32),
            pltpu.VMEM((4, D, HALF), BF16),
            pltpu.VMEM((HALF, D), BF16),
            pltpu.VMEM((4, 2, BLK, HALF), BF16),
            pltpu.VMEM((4, 2, BLK, HALF), F32),
            heads,
            heads,
            heads,
            heads,
            pltpu.VMEM((3, HEADS * BLK, BLK), BF16),
            pltpu.VMEM((3, HEADS * BLK, BLK), F32),
            pltpu.VMEM((2, BLK, HALF), F32),
            pltpu.VMEM((4, SEQ, HALF), BF16),
            pltpu.VMEM((SEQ, 128), F32),
            pltpu.VMEM((SEQ, 128), F32),
            pltpu.VMEM((2, BLK, D), F32),
            pltpu.VMEM((BLK, D), F32),
            pltpu.VMEM((2, BLK, D), F32),
            pltpu.VMEM((BLK, D), F32),
            pltpu.VMEM((2, 8, 128), F32),
            pltpu.VMEM((4, 8, 128), F32),
            pltpu.VMEM((8, 8, 128), F32),
            pltpu.VMEM((8, 8, 128), F32),
            dma((9,)),
            dma((LEVELS * ns,)),
            dma((LEVELS * ns,)),
            dma((6,)),
            dma((6,)),
            dma((3,)),
            dma((3,)),
            dma((ns,)),
            dma((ns,)),
        ],
        compiler_params=pltpu.CompilerParams(collective_id=1, has_side_effects=True, vmem_limit_bytes=48 << 20),
        name="layer",
    )(lengths, *operands)

    factor = 1.0 / math.sqrt(users * SEQ)
    out, grad, g_in, g_out, gain_in_grad, gain_attn_grad = pl.pallas_call(
        functools.partial(widen_kernel, factor),
        out_shape=(
            shape((BLK, D), BF16),
            shape((BLK, D), BF16),
            shape((D, 4 * D), F32),
            shape((D, D), F32),
            shape((1, D), F32),
            shape((1, D), F32),
        ),
        in_specs=[VMEM] * (3 + ns),
        out_specs=(HBM,) * 6,
        scratch_shapes=[
            pltpu.VMEM((D, 4 * D), F32),
            pltpu.VMEM((D, D), F32),
            pltpu.VMEM((2, 1, D), F32),
            dma((13,)),
        ],
        compiler_params=pltpu.CompilerParams(vmem_limit_bytes=32 << 20),
        name="widen",
    )(out, grad, gains, *results)
    return out[None], grad[None], g_in, g_out, gain_in_grad[0], gain_attn_grad[0]


def solution(mesh):
    placed = (P("dp", "ctx", None), P("dp"), P(), P(), P(), P(), P("dp", "ctx", None))
    return jax.shard_map(
        functools.partial(per_device, mesh.shape["dp"]),
        mesh=mesh,
        in_specs=placed,
        out_specs=(P("dp", "ctx", None), P("dp", "ctx", None), P(), P(), P(), P()),
        check_vma=False,
    )
```

```python
import functools
import math

import jax
import jax.numpy as jnp
from jax import lax
from jax.experimental import pallas as pl
from jax.experimental.pallas import tpu as pltpu
from jax.sharding import PartitionSpec as P

MESH = pl.DeviceIdType.MESH
F32 = jnp.float32
BF16 = jnp.bfloat16
D = 512
DH = 64
BLK = 128
SEQ = 256
HALF = 256
HEADS = 4
SIZES = (4, 8, 8)
EPS = 1e-05
SCORE_SCALE = 1.0 / math.sqrt(DH)
XYZ, XZY, YXZ, ZXY = (0, 1, 2), (0, 2, 1), (1, 0, 2), (2, 0, 1)
ROWS = 16
STREAMS = (XYZ, XZY, YXZ, ZXY, YXZ, ZXY, XYZ, XZY, XYZ, XZY)
GATING, OUT, VALUES, KEYS, QUERIES = 0, 2, 4, 6, 8
STREAM_OF = (GATING, VALUES, QUERIES, KEYS)
LEVELS = 5


def dot(left, right, dims):
    return lax.dot_general(left, right, (dims, ((), ())), preferred_element_type=F32)


def rows_dot(left, right):
    return dot(left, right, ((1,), (0,)))


def cols_dot(left, right):
    return dot(left, right, ((1,), (1,)))


def sum_rows_dot(left, right):
    return dot(left, right, ((0,), (0,)))


def sigmoid(t):
    return 0.5 * jnp.tanh(0.5 * t) + 0.5


def standardize(t):
    centered = t - jnp.mean(t, axis=-1, keepdims=True)
    rstd = lax.rsqrt(jnp.mean(centered * centered, axis=-1, keepdims=True) + EPS)
    return centered * rstd, rstd


class Place:
    def __init__(self):
        self.dp = lax.axis_index("dp")
        self.core = lax.axis_index("ctx")
        self.pos = (lax.rem(self.dp, 4), lax.rem(self.dp // 4, 8), self.dp // 32)
        self.partner = (self.dp, 1 - self.core)
        self.peers = []
        for axis, (n, stride) in enumerate(zip(SIZES, (1, 4, 32))):
            me = self.pos[axis]
            others = [lax.rem(me + d, n) for d in sorted(range(1, n), key=lambda d: -min(d, n - d))]
            self.peers.append([(k, (self.dp + (k - me) * stride, self.core)) for k in others])


def wait_bytes(region, sem):
    pltpu.make_async_copy(region, region, sem).wait()


class Stream:
    def __init__(self, place, order, bufs, result, ssem, rsem, base):
        self.place, self.order, self.base = place, order, base
        self.src, self.r1, self.s1, self.r2, self.r3 = bufs
        self.res = result
        self.ssem, self.rsem = ssem, rsem
        self.n = [SIZES[a] for a in order]
        self.me = [place.pos[a] for a in order]

    def fan(self, phase, level, src, dst):
        for k, device in self.place.peers[self.order[level]]:
            pltpu.make_async_remote_copy(
                src_ref=src(k),
                dst_ref=dst,
                send_sem=self.ssem.at[self.base + phase],
                recv_sem=self.rsem.at[self.base + phase],
                device_id=device,
                device_id_type=MESH,
            ).start()

    def wait_recv(self, phase, region):
        wait_bytes(region, self.rsem.at[self.base + phase])

    def total(self, ref, n):
        acc = ref[0].astype(F32)
        for j in range(1, n):
            acc = acc + ref[j].astype(F32)
        return acc.astype(BF16)

    def scatter1(self):
        self.fan(0, 0, lambda k: self.src.at[k], self.r1.at[self.me[0]])

    def scatter2(self):
        n, me = self.n[0], self.me[0]
        self.wait_recv(0, self.r1.at[pl.ds(0, n - 1)])
        self.r1[me] = self.src[me]
        self.s1[...] = self.total(self.r1, n)
        self.fan(1, 1, lambda k: self.s1.at[k], self.r2.at[self.me[1]])

    def exchange(self):
        n, me = self.n[1], self.me[1]
        self.wait_recv(1, self.r2.at[pl.ds(0, n - 1)])
        self.r2[me] = self.s1[me]
        own = self.r3.at[self.me[2]]
        own[...] = self.total(self.r2, n)
        self.fan(2, 2, lambda k: own, own)

    def gather2(self):
        n = self.n[2]
        self.wait_recv(2, self.r3.at[pl.ds(0, n - 1)])
        own = self.res.at[self.me[0], self.me[1]]
        own[...] = self.total(self.r3, n)
        self.fan(3, 1, lambda k: own, own)

    def gather1(self):
        own = self.res.at[self.me[0]]
        self.wait_recv(3, own.at[pl.ds(0, self.n[1] - 1)])
        self.fan(4, 0, lambda k: own, own)

    def finish(self):
        self.wait_recv(4, self.res.at[pl.ds(0, self.n[0] - 1)])

    def drain(self):
        n = self.n
        regions = (
            self.r1.at[pl.ds(0, n[0] - 1)],
            self.r2.at[pl.ds(0, n[1] - 1)],
            self.r3.at[pl.ds(0, n[2] - 1)],
            self.res.at[0, pl.ds(0, n[1] - 1)],
            self.res.at[pl.ds(0, n[0] - 1)],
        )
        for phase, region in enumerate(regions):
            wait_bytes(region, self.ssem.at[self.base + phase])


def layer_kernel(
    len_ref, hist_hbm, cot_hbm, gain_in_hbm, gain_attn_hbm, w_in_ref, w_out_ref,
    out_ref, grad_ref, gains_ref, *rest,
):
    ns = len(STREAMS)
    results, rest = rest[:ns], rest[ns:]
    stream_bufs, rest = rest[: 5 * ns], rest[5 * ns :]
    (
        hist, gains, cots, normed, normed_t, xhat_own, w_own, wo_own, hid, slope, q_heads, k_heads, v_heads, d_heads,
        weights, turn, attended, dpre, stat_own, stat_other, proj, proj_in, dnorm, dnorm_in, gx0, gx1, gx2, gx3,
        lsem, ssem, rsem, psem, qsem, gssem, grsem, fssem, frsem, relay,
    ) = rest
    place = Place()
    core = place.core
    away = 1 - core
    partner = place.partner

    near = [device for axis in (1, 2) for _, device in place.peers[axis][3:]]
    near += [device for _, device in place.peers[0]] + [partner]
    two_away = [device for axis in (1, 2) for _, device in place.peers[axis][3:5]]

    with jax.named_scope("start"):
        barrier = pltpu.get_barrier_semaphore()
        for device in near:
            pl.semaphore_signal(barrier, inc=1, device_id=device, device_id_type=MESH)
        first = pl.multiple_of(core * HALF, HALF)
        loads = [
            pltpu.make_async_copy(hist_hbm, hist, lsem.at[0]),
            pltpu.make_async_copy(gain_in_hbm, gains.at[0], lsem.at[1]),
            pltpu.make_async_copy(cot_hbm, cots.at[core], lsem.at[2]),
        ]
        w_loads = [None] * 4
        for i, g in enumerate((2, 3, 1, 0)):
            columns = pl.ds(pl.multiple_of(g * D + first, HALF), HALF)
            w_loads[g] = pltpu.make_async_copy(w_in_ref.at[:, columns], w_own.at[g], lsem.at[3 + i])
            loads.append(w_loads[g])
        wo_load = pltpu.make_async_copy(w_out_ref.at[pl.ds(first, HALF), :], wo_own, lsem.at[7])
        ga_load = pltpu.make_async_copy(gain_attn_hbm, gains.at[1], lsem.at[8])
        loads += [wo_load, ga_load]
        for load in loads:
            load.start()

    streams = [
        Stream(place, order, stream_bufs[5 * i : 5 * i + 5], results[i].at[core], ssem, rsem, LEVELS * i)
        for i, order in enumerate(STREAMS)
    ]

    def to_partner(src, dst, i):
        copy = pltpu.make_async_remote_copy(
            src_ref=src,
            dst_ref=dst,
            send_sem=psem.at[i],
            recv_sem=qsem.at[i],
            device_id=partner,
            device_id_type=MESH,
        )
        copy.start()
        return copy

    lane_head = lax.broadcasted_iota(jnp.int32, (1, HALF), 1) // DH

    def valid_rows(block):
        row = lax.broadcasted_iota(jnp.int32, (BLK, 1), 0) + block * BLK
        return (row < len_ref[0]).astype(F32)

    def put_heads(ref, block, t):
        for h in range(HEADS):
            ref[block, h * BLK : h * BLK + BLK, :] = jnp.where(lane_head == h, t, jnp.zeros_like(t))

    def heads_beside(t):
        return jnp.concatenate([t[h * BLK : h * BLK + BLK] for h in range(HEADS)], axis=1)

    def project(block, wait):
        for g in (2, 3, 1, 0):
            if wait:
                w_loads[g].wait()
            half = 0.5 * rows_dot(normed[block], w_own[g])
            t = jnp.tanh(half)
            u = half * t
            hidden = (half + u).astype(BF16)
            slope[g, block] = (0.03125 if g == 2 else 0.5) * ((1.0 + t) * (1.0 + half - u))
            if g == 2:
                put_heads(q_heads, block, hidden * (0.5 * SCORE_SCALE))
            else:
                hid[g, block] = hidden
                if g == 3:
                    put_heads(k_heads, block, hidden)
                if g == 1:
                    put_heads(v_heads, block, hidden)

    def attend(tile, q_block, k_block, diagonal):
        half = cols_dot(q_heads[q_block], hid[3, k_block])
        t = jnp.tanh(half)
        u = half * t
        weight = half + u
        turned = (1.0 + t) * (1.0 + half - u)
        if diagonal:
            q_pos = lax.broadcasted_iota(jnp.int32, (HEADS * BLK, BLK), 0) & (BLK - 1)
            k_pos = lax.broadcasted_iota(jnp.int32, (HEADS * BLK, BLK), 1)
            allowed = k_pos <= q_pos
            weight = jnp.where(allowed, weight, 0.0)
            turned = jnp.where(allowed, turned, 0.0)
        weight = weight.astype(BF16)
        weights[tile] = weight
        turn[tile] = turned
        return rows_dot(heads_beside(weight), v_heads[k_block])

    with jax.named_scope("own_project"):
        loads[0].wait()
        loads[1].wait()
        xhat, rstd_in = standardize(hist[...].astype(F32))
        xhat_own[...] = xhat
        normed[core] = (xhat * gains[0]).astype(BF16)
        project(core, True)
    with jax.named_scope("barrier"):
        loads[2].wait()
        pl.semaphore_wait(barrier, len(near))
        normed_copy = to_partner(normed.at[core], normed.at[core], 0)
        cots_copy = to_partner(cots.at[core], cots.at[core], 1)
        for device in two_away:
            pl.semaphore_signal(relay, inc=1, device_id=device, device_id_type=MESH)
    with jax.named_scope("own_attend"):
        attended[core] = attend(core, core, core, True)
    with jax.named_scope("share_wait"):
        normed_copy.wait_recv()
    with jax.named_scope("other_project"):
        project(away, False)
    with jax.named_scope("other_attend"):
        attended[away] = attend(away, away, away, True)
        attended[1] = attended[1] + attend(2, 1, 0, False)
    with jax.named_scope("d_mixed"):
        cots_copy.wait_recv()
        wo_load.wait()
        ga_load.wait()
        valid = jnp.concatenate([valid_rows(0), valid_rows(1)], axis=0)
        d_proj = (cots[...].reshape(SEQ, D).astype(F32) * valid).astype(BF16)
        gain_attn = gains[1, :, pl.ds(first, HALF)]
        att = attended[...].reshape(SEQ, HALF) * valid
        gating = hid[0].reshape(SEQ, HALF).astype(F32)
        d_mixed = cols_dot(d_proj, wo_own[...])
        g = d_mixed * gain_attn * gating
    with jax.named_scope("stats"):
        half_mean = jnp.mean(att, axis=-1, keepdims=True)
        centered = att - half_mean
        half_sq = jnp.sum(centered * centered, axis=-1, keepdims=True)
        half_g = jnp.sum(g, axis=-1, keepdims=True)
        half_gc = jnp.sum(g * centered, axis=-1, keepdims=True)
        lane = lax.broadcasted_iota(jnp.int32, (SEQ, 128), 1)
        stat_own[...] = jnp.where(
            lane == 0, half_mean, jnp.where(lane == 1, half_sq, jnp.where(lane == 2, half_g, half_gc))
        )
        stat_copy = to_partner(stat_own, stat_other, 2)
        normed_t[...] = normed[...].reshape(SEQ, D).T
    with jax.named_scope("stats_wait"):
        stat_copy.wait_recv()
    with jax.named_scope("norm"):
        other = stat_other[...]
        o_mean, o_sq, o_g, o_gc = (other[:, i : i + 1] for i in range(4))
        mean = 0.5 * (half_mean + o_mean)
        up, o_up = half_mean - mean, o_mean - mean
        var = (half_sq + o_sq + HALF * (up * up + o_up * o_up)) * (1.0 / D)
        rstd = lax.rsqrt(var + EPS)
        mean_g = (half_g + o_g) * (1.0 / D)
        mean_gn = rstd * (half_gc + o_gc + half_g * up + o_g * o_up) * (1.0 / D)
        norm = (att - mean) * rstd
        ng = norm * gain_attn
        mixed = (ng * gating).astype(BF16)
        d_att = (rstd * (g - mean_g - norm * mean_gn) * valid).astype(BF16)
        g_attn = jnp.sum(d_mixed * norm * gating, axis=0, keepdims=True)

    def put(group, halves):
        for half, part in enumerate(halves):
            stream = streams[group + half]
            stream.src[...] = part.astype(BF16).reshape(stream.n[0], stream.n[1], ROWS, 128)
            stream.scatter1()

    def columns_in_halves(t):
        return [t[:, :128], t[:, 128:]]

    def of(group):
        return streams[group : group + 2]

    def weight_grad(g, d_hidden):
        d_pre = (d_hidden * slope[g].reshape(SEQ, HALF)).astype(BF16)
        dpre[g] = d_pre
        return rows_dot(normed_t[...], d_pre)

    with jax.named_scope("grads_u"):
        put(GATING, columns_in_halves(weight_grad(0, d_mixed * ng)))
        g_out = rows_dot(mixed.T, d_proj)
        pl.semaphore_wait(relay, len(two_away))
        g_out = [g_out[:, i * 128 : i * 128 + 128] for i in range(4)]
        put(OUT, [jnp.concatenate(g_out[:2], axis=0), jnp.concatenate(g_out[2:], axis=0)])
    with jax.named_scope("grads_v"):
        for block in range(2):
            put_heads(d_heads, block, d_att[block * BLK : block * BLK + BLK])
        d_values_0 = sum_rows_dot(weights[0], d_heads[0]) + sum_rows_dot(weights[2], d_heads[1])
        d_values_1 = sum_rows_dot(weights[1], d_heads[1])
        put(VALUES, columns_in_halves(weight_grad(1, jnp.concatenate([d_values_0, d_values_1], axis=0))))
    with jax.named_scope("grads_k"):
        slopes = []
        for tile, (q_block, k_block) in enumerate(((0, 0), (1, 1), (1, 0))):
            slopes.append((cols_dot(d_heads[q_block], hid[1, k_block]) * turn[tile]).astype(BF16))
        d_keys_0 = sum_rows_dot(slopes[0], q_heads[0]) + sum_rows_dot(slopes[2], q_heads[1])
        d_keys_1 = sum_rows_dot(slopes[1], q_heads[1])
        put(KEYS, columns_in_halves(weight_grad(3, jnp.concatenate([d_keys_0, d_keys_1], axis=0))))
    with jax.named_scope("grads_q"):
        d_query_0 = rows_dot(heads_beside(slopes[0]), k_heads[0])
        d_query_1 = rows_dot(heads_beside(slopes[1]), k_heads[1]) + rows_dot(heads_beside(slopes[2]), k_heads[0])
        put(QUERIES, columns_in_halves(weight_grad(2, jnp.concatenate([d_query_0, d_query_1], axis=0))))
    with jax.named_scope("scatter2_u"):
        for s in of(GATING):
            s.scatter2()
    with jax.named_scope("d_norm"):
        d_norm = cols_dot(dpre[0], w_own[0])
        for g in range(1, 4):
            d_norm = d_norm + cols_dot(dpre[g], w_own[g])
        dnorm[...] = d_norm.reshape(2, BLK, D)
        dnorm_copy = to_partner(dnorm.at[away], dnorm_in, 3)
    with jax.named_scope("scatter2_out"):
        for s in of(OUT):
            s.scatter2()
    with jax.named_scope("proj"):
        proj[...] = rows_dot(mixed, wo_own[...]).reshape(2, BLK, D)
        proj_copy = to_partner(proj.at[away], proj_in, 4)

    with jax.named_scope("gain_sums"):
        xhat = xhat_own[...]
        dnorm_copy.wait_recv()
        d_norm = dnorm[core] + dnorm_in[...]
        gain_part = jnp.sum(d_norm * xhat, axis=0, keepdims=True)
        mine = (core == 0).astype(F32)
        gx0_own = gx0.at[core]
        for i in range(4):
            gx0_own[i : i + 1, :] = gain_part[:, i * 128 : i * 128 + 128]
        for i in range(2):
            part = g_attn[:, i * 128 : i * 128 + 128]
            gx0_own[4 + i : 5 + i, :] = part * mine
            gx0_own[6 + i : 7 + i, :] = part * (1.0 - mine)
        gain_copy = to_partner(gx0_own, gx0_own, 5)

    def gains_fan(axis, buf):
        own = buf.at[place.pos[axis]]
        for _, device in place.peers[axis]:
            pltpu.make_async_remote_copy(
                src_ref=own,
                dst_ref=own,
                send_sem=gssem.at[axis],
                recv_sem=grsem.at[axis],
                device_id=device,
                device_id_type=MESH,
            ).start()

    def gains_total(axis, buf):
        n = SIZES[axis]
        wait_bytes(buf.at[pl.ds(0, n - 1)], grsem.at[axis])
        acc = buf[0]
        for j in range(1, n):
            acc = acc + buf[j]
        return acc

    with jax.named_scope("scatter2_rest"):
        for s in of(KEYS) + of(QUERIES) + of(VALUES):
            s.scatter2()
    with jax.named_scope("gains_x"):
        gain_copy.wait_recv()
        gx1[place.pos[0]] = gx0[0] + gx0[1]
        gains_fan(0, gx1)

    with jax.named_scope("grad_history"):
        e = d_norm * gains[0]
        d_hist = rstd_in * (
            e - jnp.mean(e, axis=-1, keepdims=True) - xhat * jnp.mean(e * xhat, axis=-1, keepdims=True)
        )
        grad_ref[...] = (cots[core].astype(F32) + d_hist).astype(BF16)
        proj_copy.wait_recv()
        out_ref[...] = (hist[...].astype(F32) + valid_rows(core) * (proj[core] + proj_in[...])).astype(BF16)

    with jax.named_scope("exchange_first"):
        for s in of(GATING) + of(OUT):
            s.exchange()
    with jax.named_scope("exchange_rest"):
        for s in of(KEYS) + of(VALUES) + of(QUERIES):
            s.exchange()
    with jax.named_scope("gains_y"):
        gx2[place.pos[1]] = gains_total(0, gx1)
        gains_fan(1, gx2)
    with jax.named_scope("gather2_first"):
        for s in of(GATING) + of(OUT):
            s.gather2()
    with jax.named_scope("gather2_rest"):
        for s in of(KEYS) + of(VALUES) + of(QUERIES):
            s.gather2()
    with jax.named_scope("gains_z"):
        gx3[place.pos[2]] = gains_total(1, gx2)
        gains_fan(2, gx3)
    order = of(OUT) + of(GATING) + of(VALUES) + of(KEYS) + of(QUERIES)
    with jax.named_scope("gather1"):
        for s in order:
            s.gather1()
    with jax.named_scope("gains_end"):
        gains_ref[...] = gains_total(2, gx3)
    with jax.named_scope("finish"):
        forwards = []
        for i, s in enumerate(order):
            s.finish()
            forwards.append(
                pltpu.make_async_remote_copy(
                    src_ref=s.res,
                    dst_ref=s.res,
                    send_sem=fssem.at[i],
                    recv_sem=frsem.at[i],
                    device_id=partner,
                    device_id_type=MESH,
                )
            )
            forwards[-1].start()
    with jax.named_scope("drain"):
        for axis, buf in enumerate((gx1, gx2, gx3)):
            wait_bytes(buf.at[pl.ds(0, SIZES[axis] - 1)], gssem.at[axis])
        for copy in (normed_copy, cots_copy, stat_copy, dnorm_copy, proj_copy, gain_copy):
            copy.wait_send()
        for s in streams:
            s.drain()
        for copy in forwards:
            copy.wait()


def widen_kernel(factor, *refs):
    ns = len(STREAMS)
    out_in, grad_in, gains_ref, results = refs[0], refs[1], refs[2], refs[3 : 3 + ns]
    out_ref, grad_ref, w_in_ref, w_out_ref, gin_ref, gattn_ref, w_in_wide, w_out_wide, gains_wide, sem = refs[3 + ns :]
    copies = []

    def send(src, dst):
        copies.append(pltpu.make_async_copy(src, dst, sem.at[len(copies)]))
        copies[-1].start()

    def wide(t):
        return t.astype(F32) * factor

    for half in range(2):
        for core in range(2):
            part = wide(results[OUT + half][core].reshape(D, 128))
            for i in range(2):
                column = (2 * half + i) * 128
                w_out_wide[core * HALF : core * HALF + HALF, column : column + 128] = part[i * HALF : i * HALF + HALF]
    send(w_out_wide, w_out_ref)
    for g in range(4):
        for core in range(2):
            for half in range(2):
                column = (4 * g + 2 * core + half) * 128
                part = results[STREAM_OF[g] + half][core].reshape(D, 128)
                w_in_wide[:, column : column + 128] = wide(part)
            columns = slice((4 * g + 2 * core) * 128, (4 * g + 2 * core + 2) * 128)
            send(w_in_wide.at[:, columns], w_in_ref.at[:, columns])
    for i in range(4):
        gains_wide[0, :, i * 128 : i * 128 + 128] = gains_ref[i : i + 1, :] * factor
        gains_wide[1, :, i * 128 : i * 128 + 128] = gains_ref[4 + i : 5 + i, :] * factor
    send(gains_wide.at[0], gin_ref)
    send(gains_wide.at[1], gattn_ref)
    send(out_in, out_ref)
    send(grad_in, grad_ref)
    for copy in copies:
        copy.wait()


VMEM = pl.BlockSpec(memory_space=pltpu.VMEM)
SMEM = pl.BlockSpec(memory_space=pltpu.SMEM)
HBM = pl.BlockSpec(memory_space=pltpu.HBM)


def shape(dims, kind):
    return jax.ShapeDtypeStruct(dims, kind)


def per_device(users, history, lengths, input_gain, gain_attn, w_in, w_out, cotangent):
    history, cotangent = history[0], cotangent[0]
    input_gain, gain_attn = input_gain[None], gain_attn[None]
    operands = [history, cotangent, input_gain, gain_attn, w_in, w_out]
    operands = [pltpu.with_memory_space_constraint(t, pltpu.HBM) for t in operands]
    dma = pltpu.SemaphoreType.DMA

    buffers, result_shapes = [], []
    for order in STREAMS:
        n = [SIZES[a] for a in order]
        result_shapes.append(shape((2, n[0], n[1], ROWS, 128), BF16))
        buffers += [
            pltpu.VMEM((n[0], n[1], ROWS, 128), BF16),
            pltpu.VMEM((n[0], n[1], ROWS, 128), BF16),
            pltpu.VMEM((n[1], ROWS, 128), BF16),
            pltpu.VMEM((n[1], ROWS, 128), BF16),
            pltpu.VMEM((n[2], ROWS, 128), BF16),
        ]
    ns = len(STREAMS)
    heads = pltpu.VMEM((2, HEADS * BLK, HALF), BF16)
    out, grad, gains, *results = pl.pallas_call(
        layer_kernel,
        out_shape=(shape((BLK, D), BF16), shape((BLK, D), BF16), shape((8, 128), F32), *result_shapes),
        in_specs=[SMEM] + [HBM] * 6,
        out_specs=(VMEM,) * (3 + ns),
        scratch_shapes=buffers
        + [
            pltpu.VMEM((BLK, D), BF16),
            pltpu.VMEM((2, 1, D), F32),
            pltpu.VMEM((2, BLK, D), BF16),
            pltpu.VMEM((2, BLK, D), BF16),
            pltpu.VMEM((D, SEQ), BF16),
            pltpu.VMEM((BLK, D), F32),
            pltpu.VMEM((4, D, HALF), BF16),
            pltpu.VMEM((HALF, D), BF16),
            pltpu.VMEM((4, 2, BLK, HALF), BF16),
            pltpu.VMEM((4, 2, BLK, HALF), F32),
            heads,
            heads,
            heads,
            heads,
            pltpu.VMEM((3, HEADS * BLK, BLK), BF16),
            pltpu.VMEM((3, HEADS * BLK, BLK), F32),
            pltpu.VMEM((2, BLK, HALF), F32),
            pltpu.VMEM((4, SEQ, HALF), BF16),
            pltpu.VMEM((SEQ, 128), F32),
            pltpu.VMEM((SEQ, 128), F32),
            pltpu.VMEM((2, BLK, D), F32),
            pltpu.VMEM((BLK, D), F32),
            pltpu.VMEM((2, BLK, D), F32),
            pltpu.VMEM((BLK, D), F32),
            pltpu.VMEM((2, 8, 128), F32),
            pltpu.VMEM((4, 8, 128), F32),
            pltpu.VMEM((8, 8, 128), F32),
            pltpu.VMEM((8, 8, 128), F32),
            dma((9,)),
            dma((LEVELS * ns,)),
            dma((LEVELS * ns,)),
            dma((6,)),
            dma((6,)),
            dma((3,)),
            dma((3,)),
            dma((ns,)),
            dma((ns,)),
            pltpu.SemaphoreType.REGULAR,
        ],
        compiler_params=pltpu.CompilerParams(collective_id=1, has_side_effects=True, vmem_limit_bytes=48 << 20),
        name="layer",
    )(lengths, *operands)

    factor = 1.0 / math.sqrt(users * SEQ)
    out, grad, g_in, g_out, gain_in_grad, gain_attn_grad = pl.pallas_call(
        functools.partial(widen_kernel, factor),
        out_shape=(
            shape((BLK, D), BF16),
            shape((BLK, D), BF16),
            shape((D, 4 * D), F32),
            shape((D, D), F32),
            shape((1, D), F32),
            shape((1, D), F32),
        ),
        in_specs=[VMEM] * (3 + ns),
        out_specs=(HBM,) * 6,
        scratch_shapes=[
            pltpu.VMEM((D, 4 * D), F32),
            pltpu.VMEM((D, D), F32),
            pltpu.VMEM((2, 1, D), F32),
            dma((13,)),
        ],
        compiler_params=pltpu.CompilerParams(vmem_limit_bytes=32 << 20),
        name="widen",
    )(out, grad, gains, *results)
    return out[None], grad[None], g_in, g_out, gain_in_grad[0], gain_attn_grad[0]


def solution(mesh):
    placed = (P("dp", "ctx", None), P("dp"), P(), P(), P(), P(), P("dp", "ctx", None))
    return jax.shard_map(
        functools.partial(per_device, mesh.shape["dp"]),
        mesh=mesh,
        in_specs=placed,
        out_specs=(P("dp", "ctx", None), P("dp", "ctx", None), P(), P(), P(), P()),
        check_vma=False,
    )
```

```python
import functools
import math

import jax
import jax.numpy as jnp
from jax import lax
from jax.experimental import pallas as pl
from jax.experimental.pallas import tpu as pltpu
from jax.sharding import PartitionSpec as P

MESH = pl.DeviceIdType.MESH
F32 = jnp.float32
BF16 = jnp.bfloat16
D = 512
DH = 64
BLK = 128
SEQ = 256
HALF = 256
HEADS = 4
SIZES = (4, 8, 8)
EPS = 1e-05
SCORE_SCALE = 1.0 / math.sqrt(DH)
XYZ, XZY, YXZ, ZXY = (0, 1, 2), (0, 2, 1), (1, 0, 2), (2, 0, 1)
ROWS = 16
STREAMS = (XYZ, XZY, YXZ, ZXY, YXZ, ZXY, XYZ, XZY, XYZ, XZY)
GATING, OUT, VALUES, KEYS, QUERIES = 0, 2, 4, 6, 8
STREAM_OF = (GATING, VALUES, QUERIES, KEYS)
LEVELS = 5


def dot(left, right, dims):
    return lax.dot_general(left, right, (dims, ((), ())), preferred_element_type=F32)


def rows_dot(left, right):
    return dot(left, right, ((1,), (0,)))


def cols_dot(left, right):
    return dot(left, right, ((1,), (1,)))


def sum_rows_dot(left, right):
    return dot(left, right, ((0,), (0,)))


def sigmoid(t):
    return 0.5 * jnp.tanh(0.5 * t) + 0.5


def standardize(t):
    centered = t - jnp.mean(t, axis=-1, keepdims=True)
    rstd = lax.rsqrt(jnp.mean(centered * centered, axis=-1, keepdims=True) + EPS)
    return centered * rstd, rstd


class Place:
    def __init__(self):
        self.dp = lax.axis_index("dp")
        self.core = lax.axis_index("ctx")
        self.pos = (lax.rem(self.dp, 4), lax.rem(self.dp // 4, 8), self.dp // 32)
        self.partner = (self.dp, 1 - self.core)
        self.peers = []
        for axis, (n, stride) in enumerate(zip(SIZES, (1, 4, 32))):
            me = self.pos[axis]
            others = [lax.rem(me + d, n) for d in sorted(range(1, n), key=lambda d: -min(d, n - d))]
            self.peers.append([(k, (self.dp + (k - me) * stride, self.core)) for k in others])


def wait_bytes(region, sem):
    pltpu.make_async_copy(region, region, sem).wait()


class Stream:
    def __init__(self, place, order, bufs, result, ssem, rsem, base):
        self.place, self.order, self.base = place, order, base
        self.src, self.r1, self.s1, self.r2, self.r3 = bufs
        self.res = result
        self.ssem, self.rsem = ssem, rsem
        self.n = [SIZES[a] for a in order]
        self.me = [place.pos[a] for a in order]

    def fan(self, phase, level, src, dst):
        for k, device in self.place.peers[self.order[level]]:
            pltpu.make_async_remote_copy(
                src_ref=src(k),
                dst_ref=dst,
                send_sem=self.ssem.at[self.base + phase],
                recv_sem=self.rsem.at[self.base + phase],
                device_id=device,
                device_id_type=MESH,
            ).start()

    def wait_recv(self, phase, region):
        wait_bytes(region, self.rsem.at[self.base + phase])

    def total(self, ref, n):
        acc = ref[0].astype(F32)
        for j in range(1, n):
            acc = acc + ref[j].astype(F32)
        return acc.astype(BF16)

    def scatter1(self):
        self.fan(0, 0, lambda k: self.src.at[k], self.r1.at[self.me[0]])

    def scatter2(self):
        n, me = self.n[0], self.me[0]
        self.wait_recv(0, self.r1.at[pl.ds(0, n - 1)])
        self.r1[me] = self.src[me]
        self.s1[...] = self.total(self.r1, n)
        self.fan(1, 1, lambda k: self.s1.at[k], self.r2.at[self.me[1]])

    def exchange(self):
        n, me = self.n[1], self.me[1]
        self.wait_recv(1, self.r2.at[pl.ds(0, n - 1)])
        self.r2[me] = self.s1[me]
        own = self.r3.at[self.me[2]]
        own[...] = self.total(self.r2, n)
        self.fan(2, 2, lambda k: own, own)

    def gather2(self):
        n = self.n[2]
        self.wait_recv(2, self.r3.at[pl.ds(0, n - 1)])
        own = self.res.at[self.me[0], self.me[1]]
        own[...] = self.total(self.r3, n)
        self.fan(3, 1, lambda k: own, own)

    def gather1(self):
        own = self.res.at[self.me[0]]
        self.wait_recv(3, own.at[pl.ds(0, self.n[1] - 1)])
        self.fan(4, 0, lambda k: own, own)

    def finish(self):
        self.wait_recv(4, self.res.at[pl.ds(0, self.n[0] - 1)])

    def drain(self):
        n = self.n
        regions = (
            self.r1.at[pl.ds(0, n[0] - 1)],
            self.r2.at[pl.ds(0, n[1] - 1)],
            self.r3.at[pl.ds(0, n[2] - 1)],
            self.res.at[0, pl.ds(0, n[1] - 1)],
            self.res.at[pl.ds(0, n[0] - 1)],
        )
        for phase, region in enumerate(regions):
            wait_bytes(region, self.ssem.at[self.base + phase])


def layer_kernel(
    len_ref, hist_hbm, cot_hbm, gain_in_hbm, gain_attn_hbm, w_in_ref, w_out_ref,
    out_ref, grad_ref, gains_ref, *rest,
):
    ns = len(STREAMS)
    results, rest = rest[:ns], rest[ns:]
    stream_bufs, rest = rest[: 5 * ns], rest[5 * ns :]
    (
        hist, gains, cots, normed, normed_t, xhat_own, w_own, wo_own, hid, slope, q_heads, k_heads, v_heads, d_heads,
        weights, turn, attended, dpre, stat_own, stat_other, proj, proj_in, dnorm, dnorm_in, gx0, gx1, gx2, gx3,
        lsem, ssem, rsem, psem, qsem, gssem, grsem, fssem, frsem, relay,
    ) = rest
    place = Place()
    core = place.core
    away = 1 - core
    partner = place.partner

    near = [device for axis in (1, 2) for _, device in place.peers[axis][3:]]
    near += [device for _, device in place.peers[0]] + [partner]
    two_away = [device for axis in (1, 2) for _, device in place.peers[axis][3:5]]

    with jax.named_scope("start"):
        barrier = pltpu.get_barrier_semaphore()
        for device in near:
            pl.semaphore_signal(barrier, inc=1, device_id=device, device_id_type=MESH)
        first = pl.multiple_of(core * HALF, HALF)
        loads = [
            pltpu.make_async_copy(hist_hbm, hist, lsem.at[0]),
            pltpu.make_async_copy(gain_in_hbm, gains.at[0], lsem.at[1]),
            pltpu.make_async_copy(cot_hbm, cots.at[core], lsem.at[2]),
        ]
        w_loads = [None] * 4
        for i, g in enumerate((2, 3, 1, 0)):
            columns = pl.ds(pl.multiple_of(g * D + first, HALF), HALF)
            w_loads[g] = pltpu.make_async_copy(w_in_ref.at[:, columns], w_own.at[g], lsem.at[3 + i])
            loads.append(w_loads[g])
        wo_load = pltpu.make_async_copy(w_out_ref.at[pl.ds(first, HALF), :], wo_own, lsem.at[7])
        ga_load = pltpu.make_async_copy(gain_attn_hbm, gains.at[1], lsem.at[8])
        loads += [wo_load, ga_load]
        for load in loads:
            load.start()

    streams = [
        Stream(place, order, stream_bufs[5 * i : 5 * i + 5], results[i].at[core], ssem, rsem, LEVELS * i)
        for i, order in enumerate(STREAMS)
    ]

    def to_partner(src, dst, i):
        copy = pltpu.make_async_remote_copy(
            src_ref=src,
            dst_ref=dst,
            send_sem=psem.at[i],
            recv_sem=qsem.at[i],
            device_id=partner,
            device_id_type=MESH,
        )
        copy.start()
        return copy

    lane_head = lax.broadcasted_iota(jnp.int32, (1, HALF), 1) // DH

    def valid_rows(block):
        row = lax.broadcasted_iota(jnp.int32, (BLK, 1), 0) + block * BLK
        return (row < len_ref[0]).astype(F32)

    def put_heads(ref, block, t):
        for h in range(HEADS):
            ref[block, h * BLK : h * BLK + BLK, :] = jnp.where(lane_head == h, t, jnp.zeros_like(t))

    def heads_beside(t):
        return jnp.concatenate([t[h * BLK : h * BLK + BLK] for h in range(HEADS)], axis=1)

    def project(block, wait):
        for g in (2, 3, 1, 0):
            if wait:
                w_loads[g].wait()
            half = 0.5 * rows_dot(normed[block], w_own[g])
            t = jnp.tanh(half)
            u = half * t
            hidden = (half + u).astype(BF16)
            slope[g, block] = (0.03125 if g == 2 else 0.5) * ((1.0 + t) * (1.0 + half - u))
            if g == 2:
                put_heads(q_heads, block, hidden * (0.5 * SCORE_SCALE))
            else:
                hid[g, block] = hidden
                if g == 3:
                    put_heads(k_heads, block, hidden)
                if g == 1:
                    put_heads(v_heads, block, hidden)

    def attend(tile, q_block, k_block, diagonal):
        half = cols_dot(q_heads[q_block], hid[3, k_block])
        t = jnp.tanh(half)
        u = half * t
        weight = half + u
        turned = (1.0 + t) * (1.0 + half - u)
        if diagonal:
            q_pos = lax.broadcasted_iota(jnp.int32, (HEADS * BLK, BLK), 0) & (BLK - 1)
            k_pos = lax.broadcasted_iota(jnp.int32, (HEADS * BLK, BLK), 1)
            allowed = k_pos <= q_pos
            weight = jnp.where(allowed, weight, 0.0)
            turned = jnp.where(allowed, turned, 0.0)
        weight = weight.astype(BF16)
        weights[tile] = weight
        turn[tile] = turned
        return rows_dot(heads_beside(weight), v_heads[k_block])

    with jax.named_scope("own_project"):
        loads[0].wait()
        loads[1].wait()
        xhat, rstd_in = standardize(hist[...].astype(F32))
        xhat_own[...] = xhat
        normed[core] = (xhat * gains[0]).astype(BF16)
        project(core, True)
    with jax.named_scope("barrier"):
        loads[2].wait()
        pl.semaphore_wait(barrier, len(near))
        normed_copy = to_partner(normed.at[core], normed.at[core], 0)
        cots_copy = to_partner(cots.at[core], cots.at[core], 1)
        for device in two_away:
            pl.semaphore_signal(relay, inc=1, device_id=device, device_id_type=MESH)
    with jax.named_scope("own_attend"):
        attended[core] = attend(core, core, core, True)
    with jax.named_scope("share_wait"):
        normed_copy.wait_recv()
    with jax.named_scope("other_project"):
        project(away, False)
    with jax.named_scope("other_attend"):
        attended[away] = attend(away, away, away, True)
        attended[1] = attended[1] + attend(2, 1, 0, False)
    with jax.named_scope("d_mixed"):
        cots_copy.wait_recv()
        wo_load.wait()
        ga_load.wait()
        valid = jnp.concatenate([valid_rows(0), valid_rows(1)], axis=0)
        d_proj = (cots[...].reshape(SEQ, D).astype(F32) * valid).astype(BF16)
        gain_attn = gains[1, :, pl.ds(first, HALF)]
        att = attended[...].reshape(SEQ, HALF) * valid
        gating = hid[0].reshape(SEQ, HALF).astype(F32)
        d_mixed = cols_dot(d_proj, wo_own[...])
        g = d_mixed * gain_attn * gating
    with jax.named_scope("stats"):
        half_mean = jnp.mean(att, axis=-1, keepdims=True)
        centered = att - half_mean
        half_sq = jnp.sum(centered * centered, axis=-1, keepdims=True)
        half_g = jnp.sum(g, axis=-1, keepdims=True)
        half_gc = jnp.sum(g * centered, axis=-1, keepdims=True)
        lane = lax.broadcasted_iota(jnp.int32, (SEQ, 128), 1)
        stat_own[...] = jnp.where(
            lane == 0, half_mean, jnp.where(lane == 1, half_sq, jnp.where(lane == 2, half_g, half_gc))
        )
        stat_copy = to_partner(stat_own, stat_other, 2)
        normed_t[...] = normed[...].reshape(SEQ, D).T
    with jax.named_scope("stats_wait"):
        stat_copy.wait_recv()
    with jax.named_scope("norm"):
        other = stat_other[...]
        o_mean, o_sq, o_g, o_gc = (other[:, i : i + 1] for i in range(4))
        mean = 0.5 * (half_mean + o_mean)
        up, o_up = half_mean - mean, o_mean - mean
        var = (half_sq + o_sq + HALF * (up * up + o_up * o_up)) * (1.0 / D)
        rstd = lax.rsqrt(var + EPS)
        mean_g = (half_g + o_g) * (1.0 / D)
        mean_gn = rstd * (half_gc + o_gc + half_g * up + o_g * o_up) * (1.0 / D)
        norm = (att - mean) * rstd
        ng = norm * gain_attn
        mixed = (ng * gating).astype(BF16)
        d_att = (rstd * (g - mean_g - norm * mean_gn) * valid).astype(BF16)
        g_attn = jnp.sum(d_mixed * norm * gating, axis=0, keepdims=True)

    def put(group, halves):
        for half, part in enumerate(halves):
            stream = streams[group + half]
            stream.src[...] = part.astype(BF16).reshape(stream.n[0], stream.n[1], ROWS, 128)
            stream.scatter1()

    def columns_in_halves(t):
        return [t[:, :128], t[:, 128:]]

    def of(group):
        return streams[group : group + 2]

    def weight_grad(g, d_hidden):
        d_pre = (d_hidden * slope[g].reshape(SEQ, HALF)).astype(BF16)
        dpre[g] = d_pre
        return rows_dot(normed_t[...], d_pre)

    with jax.named_scope("grads_u"):
        put(GATING, columns_in_halves(weight_grad(0, d_mixed * ng)))
        g_out = rows_dot(mixed.T, d_proj)
        pl.semaphore_wait(relay, len(two_away))
        g_out = [g_out[:, i * 128 : i * 128 + 128] for i in range(4)]
        put(OUT, [jnp.concatenate(g_out[:2], axis=0), jnp.concatenate(g_out[2:], axis=0)])
    with jax.named_scope("grads_v"):
        for block in range(2):
            put_heads(d_heads, block, d_att[block * BLK : block * BLK + BLK])
        d_values_0 = sum_rows_dot(weights[0], d_heads[0]) + sum_rows_dot(weights[2], d_heads[1])
        d_values_1 = sum_rows_dot(weights[1], d_heads[1])
        put(VALUES, columns_in_halves(weight_grad(1, jnp.concatenate([d_values_0, d_values_1], axis=0))))
    with jax.named_scope("grads_k"):
        slopes = []
        for tile, (q_block, k_block) in enumerate(((0, 0), (1, 1), (1, 0))):
            slopes.append((cols_dot(d_heads[q_block], hid[1, k_block]) * turn[tile]).astype(BF16))
        d_keys_0 = sum_rows_dot(slopes[0], q_heads[0]) + sum_rows_dot(slopes[2], q_heads[1])
        d_keys_1 = sum_rows_dot(slopes[1], q_heads[1])
        put(KEYS, columns_in_halves(weight_grad(3, jnp.concatenate([d_keys_0, d_keys_1], axis=0))))
    with jax.named_scope("grads_q"):
        d_query_0 = rows_dot(heads_beside(slopes[0]), k_heads[0])
        d_query_1 = rows_dot(heads_beside(slopes[1]), k_heads[1]) + rows_dot(heads_beside(slopes[2]), k_heads[0])
        put(QUERIES, columns_in_halves(weight_grad(2, jnp.concatenate([d_query_0, d_query_1], axis=0))))
    def gains_fan(axis, buf):
        own = buf.at[place.pos[axis]]
        for _, device in place.peers[axis]:
            pltpu.make_async_remote_copy(
                src_ref=own,
                dst_ref=own,
                send_sem=gssem.at[axis],
                recv_sem=grsem.at[axis],
                device_id=device,
                device_id_type=MESH,
            ).start()

    def gains_total(axis, buf):
        n = SIZES[axis]
        wait_bytes(buf.at[pl.ds(0, n - 1)], grsem.at[axis])
        acc = buf[0]
        for j in range(1, n):
            acc = acc + buf[j]
        return acc

    order = of(OUT) + of(GATING) + of(VALUES) + of(KEYS) + of(QUERIES)
    with jax.named_scope("d_norm"):
        d_norm = cols_dot(dpre[0], w_own[0])
        for g in range(1, 4):
            d_norm = d_norm + cols_dot(dpre[g], w_own[g])
        dnorm[...] = d_norm.reshape(2, BLK, D)
        dnorm_copy = to_partner(dnorm.at[away], dnorm_in, 3)
    with jax.named_scope("proj"):
        proj[...] = rows_dot(mixed, wo_own[...]).reshape(2, BLK, D)
        proj_copy = to_partner(proj.at[away], proj_in, 4)

    with jax.named_scope("scatter2_u"):
        for s in of(GATING):
            s.scatter2()
    with jax.named_scope("gain_sums"):
        xhat = xhat_own[...]
        dnorm_copy.wait_recv()
        d_norm = dnorm[core] + dnorm_in[...]
        gain_part = jnp.sum(d_norm * xhat, axis=0, keepdims=True)
        mine = (core == 0).astype(F32)
        gx0_own = gx0.at[core]
        for i in range(4):
            gx0_own[i : i + 1, :] = gain_part[:, i * 128 : i * 128 + 128]
        for i in range(2):
            part = g_attn[:, i * 128 : i * 128 + 128]
            gx0_own[4 + i : 5 + i, :] = part * mine
            gx0_own[6 + i : 7 + i, :] = part * (1.0 - mine)
        gain_copy = to_partner(gx0_own, gx0_own, 5)

    with jax.named_scope("grad_history"):
        e = d_norm * gains[0]
        d_hist = rstd_in * (
            e - jnp.mean(e, axis=-1, keepdims=True) - xhat * jnp.mean(e * xhat, axis=-1, keepdims=True)
        )
        grad_ref[...] = (cots[core].astype(F32) + d_hist).astype(BF16)
        proj_copy.wait_recv()
        out_ref[...] = (hist[...].astype(F32) + valid_rows(core) * (proj[core] + proj_in[...])).astype(BF16)

    with jax.named_scope("scatter2_out"):
        for s in of(OUT):
            s.scatter2()
    with jax.named_scope("gains_x"):
        gain_copy.wait_recv()
        gx1[place.pos[0]] = gx0[0] + gx0[1]
        gains_fan(0, gx1)

    with jax.named_scope("scatter2_rest"):
        for s in of(KEYS) + of(QUERIES) + of(VALUES):
            s.scatter2()
    with jax.named_scope("exchange_first"):
        for s in of(GATING) + of(OUT):
            s.exchange()
    with jax.named_scope("gains_y"):
        gx2[place.pos[1]] = gains_total(0, gx1)
        gains_fan(1, gx2)
    with jax.named_scope("exchange_rest"):
        for s in of(KEYS) + of(VALUES) + of(QUERIES):
            s.exchange()
    with jax.named_scope("gather2_first"):
        for s in of(GATING) + of(OUT):
            s.gather2()
    with jax.named_scope("gains_z"):
        gx3[place.pos[2]] = gains_total(1, gx2)
        gains_fan(2, gx3)
    with jax.named_scope("gather2_rest"):
        for s in of(KEYS) + of(VALUES) + of(QUERIES):
            s.gather2()
    with jax.named_scope("gather1"):
        for s in order:
            s.gather1()
    with jax.named_scope("finish"):
        forwards = []
        for i, s in enumerate(order):
            s.finish()
            forwards.append(
                pltpu.make_async_remote_copy(
                    src_ref=s.res,
                    dst_ref=s.res,
                    send_sem=fssem.at[i],
                    recv_sem=frsem.at[i],
                    device_id=partner,
                    device_id_type=MESH,
                )
            )
            forwards[-1].start()
    with jax.named_scope("gains_end"):
        gains_ref[...] = gains_total(2, gx3)
    with jax.named_scope("drain"):
        for axis, buf in enumerate((gx1, gx2, gx3)):
            wait_bytes(buf.at[pl.ds(0, SIZES[axis] - 1)], gssem.at[axis])
        for copy in (normed_copy, cots_copy, stat_copy, dnorm_copy, proj_copy, gain_copy):
            copy.wait_send()
        for s in streams:
            s.drain()
        for copy in forwards:
            copy.wait()


def widen_kernel(factor, *refs):
    ns = len(STREAMS)
    out_in, grad_in, gains_ref, results = refs[0], refs[1], refs[2], refs[3 : 3 + ns]
    out_ref, grad_ref, w_in_ref, w_out_ref, gin_ref, gattn_ref, w_in_wide, w_out_wide, gains_wide, sem = refs[3 + ns :]
    copies = []

    def send(src, dst):
        copies.append(pltpu.make_async_copy(src, dst, sem.at[len(copies)]))
        copies[-1].start()

    def wide(t):
        return t.astype(F32) * factor

    for half in range(2):
        for core in range(2):
            part = wide(results[OUT + half][core].reshape(D, 128))
            for i in range(2):
                column = (2 * half + i) * 128
                w_out_wide[core * HALF : core * HALF + HALF, column : column + 128] = part[i * HALF : i * HALF + HALF]
    send(w_out_wide, w_out_ref)
    for g in range(4):
        for core in range(2):
            for half in range(2):
                column = (4 * g + 2 * core + half) * 128
                part = results[STREAM_OF[g] + half][core].reshape(D, 128)
                w_in_wide[:, column : column + 128] = wide(part)
            columns = slice((4 * g + 2 * core) * 128, (4 * g + 2 * core + 2) * 128)
            send(w_in_wide.at[:, columns], w_in_ref.at[:, columns])
    for i in range(4):
        gains_wide[0, :, i * 128 : i * 128 + 128] = gains_ref[i : i + 1, :] * factor
        gains_wide[1, :, i * 128 : i * 128 + 128] = gains_ref[4 + i : 5 + i, :] * factor
    send(gains_wide.at[0], gin_ref)
    send(gains_wide.at[1], gattn_ref)
    send(out_in, out_ref)
    send(grad_in, grad_ref)
    for copy in copies:
        copy.wait()


VMEM = pl.BlockSpec(memory_space=pltpu.VMEM)
SMEM = pl.BlockSpec(memory_space=pltpu.SMEM)
HBM = pl.BlockSpec(memory_space=pltpu.HBM)


def shape(dims, kind):
    return jax.ShapeDtypeStruct(dims, kind)


def per_device(users, history, lengths, input_gain, gain_attn, w_in, w_out, cotangent):
    history, cotangent = history[0], cotangent[0]
    input_gain, gain_attn = input_gain[None], gain_attn[None]
    operands = [history, cotangent, input_gain, gain_attn, w_in, w_out]
    operands = [pltpu.with_memory_space_constraint(t, pltpu.HBM) for t in operands]
    dma = pltpu.SemaphoreType.DMA

    buffers, result_shapes = [], []
    for order in STREAMS:
        n = [SIZES[a] for a in order]
        result_shapes.append(shape((2, n[0], n[1], ROWS, 128), BF16))
        buffers += [
            pltpu.VMEM((n[0], n[1], ROWS, 128), BF16),
            pltpu.VMEM((n[0], n[1], ROWS, 128), BF16),
            pltpu.VMEM((n[1], ROWS, 128), BF16),
            pltpu.VMEM((n[1], ROWS, 128), BF16),
            pltpu.VMEM((n[2], ROWS, 128), BF16),
        ]
    ns = len(STREAMS)
    heads = pltpu.VMEM((2, HEADS * BLK, HALF), BF16)
    out, grad, gains, *results = pl.pallas_call(
        layer_kernel,
        out_shape=(shape((BLK, D), BF16), shape((BLK, D), BF16), shape((8, 128), F32), *result_shapes),
        in_specs=[SMEM] + [HBM] * 6,
        out_specs=(VMEM,) * (3 + ns),
        scratch_shapes=buffers
        + [
            pltpu.VMEM((BLK, D), BF16),
            pltpu.VMEM((2, 1, D), F32),
            pltpu.VMEM((2, BLK, D), BF16),
            pltpu.VMEM((2, BLK, D), BF16),
            pltpu.VMEM((D, SEQ), BF16),
            pltpu.VMEM((BLK, D), F32),
            pltpu.VMEM((4, D, HALF), BF16),
            pltpu.VMEM((HALF, D), BF16),
            pltpu.VMEM((4, 2, BLK, HALF), BF16),
            pltpu.VMEM((4, 2, BLK, HALF), F32),
            heads,
            heads,
            heads,
            heads,
            pltpu.VMEM((3, HEADS * BLK, BLK), BF16),
            pltpu.VMEM((3, HEADS * BLK, BLK), F32),
            pltpu.VMEM((2, BLK, HALF), F32),
            pltpu.VMEM((4, SEQ, HALF), BF16),
            pltpu.VMEM((SEQ, 128), F32),
            pltpu.VMEM((SEQ, 128), F32),
            pltpu.VMEM((2, BLK, D), F32),
            pltpu.VMEM((BLK, D), F32),
            pltpu.VMEM((2, BLK, D), F32),
            pltpu.VMEM((BLK, D), F32),
            pltpu.VMEM((2, 8, 128), F32),
            pltpu.VMEM((4, 8, 128), F32),
            pltpu.VMEM((8, 8, 128), F32),
            pltpu.VMEM((8, 8, 128), F32),
            dma((9,)),
            dma((LEVELS * ns,)),
            dma((LEVELS * ns,)),
            dma((6,)),
            dma((6,)),
            dma((3,)),
            dma((3,)),
            dma((ns,)),
            dma((ns,)),
            pltpu.SemaphoreType.REGULAR,
        ],
        compiler_params=pltpu.CompilerParams(collective_id=1, has_side_effects=True, vmem_limit_bytes=48 << 20),
        name="layer",
    )(lengths, *operands)

    factor = 1.0 / math.sqrt(users * SEQ)
    out, grad, g_in, g_out, gain_in_grad, gain_attn_grad = pl.pallas_call(
        functools.partial(widen_kernel, factor),
        out_shape=(
            shape((BLK, D), BF16),
            shape((BLK, D), BF16),
            shape((D, 4 * D), F32),
            shape((D, D), F32),
            shape((1, D), F32),
            shape((1, D), F32),
        ),
        in_specs=[VMEM] * (3 + ns),
        out_specs=(HBM,) * 6,
        scratch_shapes=[
            pltpu.VMEM((D, 4 * D), F32),
            pltpu.VMEM((D, D), F32),
            pltpu.VMEM((2, 1, D), F32),
            dma((13,)),
        ],
        compiler_params=pltpu.CompilerParams(vmem_limit_bytes=32 << 20),
        name="widen",
    )(out, grad, gains, *results)
    return out[None], grad[None], g_in, g_out, gain_in_grad[0], gain_attn_grad[0]


def solution(mesh):
    placed = (P("dp", "ctx", None), P("dp"), P(), P(), P(), P(), P("dp", "ctx", None))
    return jax.shard_map(
        functools.partial(per_device, mesh.shape["dp"]),
        mesh=mesh,
        in_specs=placed,
        out_specs=(P("dp", "ctx", None), P("dp", "ctx", None), P(), P(), P(), P()),
        check_vma=False,
    )
```

```python
import functools
import math

import jax
import jax.numpy as jnp
from jax import lax
from jax.experimental import pallas as pl
from jax.experimental.pallas import tpu as pltpu
from jax.sharding import PartitionSpec as P

MESH = pl.DeviceIdType.MESH
F32 = jnp.float32
BF16 = jnp.bfloat16
D = 512
DH = 64
BLK = 128
SEQ = 256
HALF = 256
HEADS = 4
SIZES = (4, 8, 8)
EPS = 1e-05
SCORE_SCALE = 1.0 / math.sqrt(DH)
XYZ, XZY, YXZ, ZXY = (0, 1, 2), (0, 2, 1), (1, 0, 2), (2, 0, 1)
ROWS = 16
STREAMS = (XYZ, XZY, YXZ, ZXY, YXZ, ZXY, XYZ, XZY, XYZ, XZY)
GATING, OUT, VALUES, KEYS, QUERIES = 0, 2, 4, 6, 8
STREAM_OF = (GATING, VALUES, QUERIES, KEYS)
LEVELS = 5


def dot(left, right, dims):
    return lax.dot_general(left, right, (dims, ((), ())), preferred_element_type=F32)


def rows_dot(left, right):
    return dot(left, right, ((1,), (0,)))


def cols_dot(left, right):
    return dot(left, right, ((1,), (1,)))


def sum_rows_dot(left, right):
    return dot(left, right, ((0,), (0,)))


def sigmoid(t):
    return 0.5 * jnp.tanh(0.5 * t) + 0.5


def standardize(t):
    centered = t - jnp.mean(t, axis=-1, keepdims=True)
    rstd = lax.rsqrt(jnp.mean(centered * centered, axis=-1, keepdims=True) + EPS)
    return centered * rstd, rstd


class Place:
    def __init__(self):
        self.dp = lax.axis_index("dp")
        self.core = lax.axis_index("ctx")
        self.pos = (lax.rem(self.dp, 4), lax.rem(self.dp // 4, 8), self.dp // 32)
        self.partner = (self.dp, 1 - self.core)
        self.peers = []
        for axis, (n, stride) in enumerate(zip(SIZES, (1, 4, 32))):
            me = self.pos[axis]
            others = [lax.rem(me + d, n) for d in sorted(range(1, n), key=lambda d: -min(d, n - d))]
            self.peers.append([(k, (self.dp + (k - me) * stride, self.core)) for k in others])


def wait_bytes(region, sem):
    pltpu.make_async_copy(region, region, sem).wait()


class Stream:
    def __init__(self, place, order, bufs, result, ssem, rsem, base):
        self.place, self.order, self.base = place, order, base
        self.src, self.r1, self.s1, self.r2, self.r3 = bufs
        self.res = result
        self.ssem, self.rsem = ssem, rsem
        self.n = [SIZES[a] for a in order]
        self.me = [place.pos[a] for a in order]

    def fan(self, phase, level, src, dst):
        for k, device in self.place.peers[self.order[level]]:
            pltpu.make_async_remote_copy(
                src_ref=src(k),
                dst_ref=dst,
                send_sem=self.ssem.at[self.base + phase],
                recv_sem=self.rsem.at[self.base + phase],
                device_id=device,
                device_id_type=MESH,
            ).start()

    def wait_recv(self, phase, region):
        wait_bytes(region, self.rsem.at[self.base + phase])

    def total(self, ref, n):
        acc = ref[0].astype(F32)
        for j in range(1, n):
            acc = acc + ref[j].astype(F32)
        return acc.astype(BF16)

    def scatter1(self):
        self.fan(0, 0, lambda k: self.src.at[k], self.r1.at[self.me[0]])

    def scatter2(self):
        n, me = self.n[0], self.me[0]
        self.wait_recv(0, self.r1.at[pl.ds(0, n - 1)])
        self.r1[me] = self.src[me]
        self.s1[...] = self.total(self.r1, n)
        self.fan(1, 1, lambda k: self.s1.at[k], self.r2.at[self.me[1]])

    def exchange(self):
        n, me = self.n[1], self.me[1]
        self.wait_recv(1, self.r2.at[pl.ds(0, n - 1)])
        self.r2[me] = self.s1[me]
        own = self.r3.at[self.me[2]]
        own[...] = self.total(self.r2, n)
        self.fan(2, 2, lambda k: own, own)

    def gather2(self):
        n = self.n[2]
        self.wait_recv(2, self.r3.at[pl.ds(0, n - 1)])
        own = self.res.at[self.me[0], self.me[1]]
        own[...] = self.total(self.r3, n)
        self.fan(3, 1, lambda k: own, own)

    def gather1(self):
        own = self.res.at[self.me[0]]
        self.wait_recv(3, own.at[pl.ds(0, self.n[1] - 1)])
        self.fan(4, 0, lambda k: own, own)

    def finish(self):
        self.wait_recv(4, self.res.at[pl.ds(0, self.n[0] - 1)])

    def drain(self):
        n = self.n
        regions = (
            self.r1.at[pl.ds(0, n[0] - 1)],
            self.r2.at[pl.ds(0, n[1] - 1)],
            self.r3.at[pl.ds(0, n[2] - 1)],
            self.res.at[0, pl.ds(0, n[1] - 1)],
            self.res.at[pl.ds(0, n[0] - 1)],
        )
        for phase, region in enumerate(regions):
            wait_bytes(region, self.ssem.at[self.base + phase])


def layer_kernel(
    len_ref, hist_hbm, cot_hbm, gain_in_hbm, gain_attn_hbm, w_in_ref, w_out_ref,
    out_ref, grad_ref, gains_ref, *rest,
):
    ns = len(STREAMS)
    results, rest = rest[:ns], rest[ns:]
    stream_bufs, rest = rest[: 5 * ns], rest[5 * ns :]
    (
        hist, gains, cots, normed, normed_t, xhat_own, w_own, wo_own, hid, slope, q_heads, k_heads, v_heads, d_heads,
        weights, turn, attended, d_proj, d_mix, dpre, stat_own, stat_other, proj, proj_in, dnorm, dnorm_in, gx0, gx1, gx2, gx3,
        lsem, ssem, rsem, psem, qsem, gssem, grsem, fssem, frsem, relay,
    ) = rest
    place = Place()
    core = place.core
    away = 1 - core
    partner = place.partner

    near = [device for axis in (1, 2) for _, device in place.peers[axis][3:]]
    near += [device for _, device in place.peers[0]] + [partner]
    two_away = [device for axis in (1, 2) for _, device in place.peers[axis][3:5]]

    with jax.named_scope("start"):
        barrier = pltpu.get_barrier_semaphore()
        for device in near:
            pl.semaphore_signal(barrier, inc=1, device_id=device, device_id_type=MESH)
        first = pl.multiple_of(core * HALF, HALF)
        loads = [
            pltpu.make_async_copy(hist_hbm, hist, lsem.at[0]),
            pltpu.make_async_copy(gain_in_hbm, gains.at[0], lsem.at[1]),
            pltpu.make_async_copy(cot_hbm, cots.at[core], lsem.at[2]),
        ]
        w_loads = [None] * 4
        for i, g in enumerate((2, 3, 1, 0)):
            columns = pl.ds(pl.multiple_of(g * D + first, HALF), HALF)
            w_loads[g] = pltpu.make_async_copy(w_in_ref.at[:, columns], w_own.at[g], lsem.at[3 + i])
            loads.append(w_loads[g])
        wo_load = pltpu.make_async_copy(w_out_ref.at[pl.ds(first, HALF), :], wo_own, lsem.at[7])
        ga_load = pltpu.make_async_copy(gain_attn_hbm, gains.at[1], lsem.at[8])
        loads += [wo_load, ga_load]
        for load in loads:
            load.start()

    streams = [
        Stream(place, order, stream_bufs[5 * i : 5 * i + 5], results[i].at[core], ssem, rsem, LEVELS * i)
        for i, order in enumerate(STREAMS)
    ]

    def to_partner(src, dst, i):
        copy = pltpu.make_async_remote_copy(
            src_ref=src,
            dst_ref=dst,
            send_sem=psem.at[i],
            recv_sem=qsem.at[i],
            device_id=partner,
            device_id_type=MESH,
        )
        copy.start()
        return copy

    lane_head = lax.broadcasted_iota(jnp.int32, (1, HALF), 1) // DH

    def valid_rows(block):
        row = lax.broadcasted_iota(jnp.int32, (BLK, 1), 0) + block * BLK
        return (row < len_ref[0]).astype(F32)

    def put_heads(ref, block, t):
        for h in range(HEADS):
            ref[block, h * BLK : h * BLK + BLK, :] = jnp.where(lane_head == h, t, jnp.zeros_like(t))

    def heads_beside(t):
        return jnp.concatenate([t[h * BLK : h * BLK + BLK] for h in range(HEADS)], axis=1)

    def project(block, wait):
        for g in (2, 3, 1, 0):
            if wait:
                w_loads[g].wait()
            half = 0.5 * rows_dot(normed[block], w_own[g])
            t = jnp.tanh(half)
            u = half * t
            hidden = (half + u).astype(BF16)
            slope[g, block] = (0.03125 if g == 2 else 0.5) * ((1.0 + t) * (1.0 + half - u))
            if g == 2:
                put_heads(q_heads, block, hidden * (0.5 * SCORE_SCALE))
            else:
                hid[g, block] = hidden
                if g == 3:
                    put_heads(k_heads, block, hidden)
                if g == 1:
                    put_heads(v_heads, block, hidden)

    def attend(tile, q_block, k_block, diagonal):
        half = cols_dot(q_heads[q_block], hid[3, k_block])
        t = jnp.tanh(half)
        u = half * t
        weight = half + u
        turned = (1.0 + t) * (1.0 + half - u)
        if diagonal:
            q_pos = lax.broadcasted_iota(jnp.int32, (HEADS * BLK, BLK), 0) & (BLK - 1)
            k_pos = lax.broadcasted_iota(jnp.int32, (HEADS * BLK, BLK), 1)
            allowed = k_pos <= q_pos
            weight = jnp.where(allowed, weight, 0.0)
            turned = jnp.where(allowed, turned, 0.0)
        weight = weight.astype(BF16)
        weights[tile] = weight
        turn[tile] = turned
        return rows_dot(heads_beside(weight), v_heads[k_block])

    def back_through_out(block):
        d_out = (cots[block].astype(F32) * valid_rows(block)).astype(BF16)
        d_proj[block] = d_out
        d_mix[block] = cols_dot(d_out, wo_own[...])

    with jax.named_scope("own_project"):
        loads[0].wait()
        loads[1].wait()
        xhat, rstd_in = standardize(hist[...].astype(F32))
        xhat_own[...] = xhat
        normed[core] = (xhat * gains[0]).astype(BF16)
        project(core, True)
    with jax.named_scope("barrier"):
        loads[2].wait()
        pl.semaphore_wait(barrier, len(near))
        normed_copy = to_partner(normed.at[core], normed.at[core], 0)
        cots_copy = to_partner(cots.at[core], cots.at[core], 1)
        for device in two_away:
            pl.semaphore_signal(relay, inc=1, device_id=device, device_id_type=MESH)
    with jax.named_scope("own_attend"):
        attended[core] = attend(core, core, core, True)
    with jax.named_scope("own_mixed"):
        wo_load.wait()
        ga_load.wait()
        gain_attn = gains[1, :, pl.ds(first, HALF)]
        back_through_out(core)
    with jax.named_scope("share_wait"):
        normed_copy.wait_recv()
    with jax.named_scope("other_project"):
        project(away, False)
    with jax.named_scope("other_attend"):
        attended[away] = attend(away, away, away, True)
        attended[1] = attended[1] + attend(2, 1, 0, False)
    with jax.named_scope("other_mixed"):
        cots_copy.wait_recv()
        back_through_out(away)
        valid = jnp.concatenate([valid_rows(0), valid_rows(1)], axis=0)
        att = attended[...].reshape(SEQ, HALF) * valid
        gating = hid[0].reshape(SEQ, HALF).astype(F32)
        d_mixed = d_mix[...].reshape(SEQ, HALF)
        g = d_mixed * gain_attn * gating
    with jax.named_scope("stats"):
        half_mean = jnp.mean(att, axis=-1, keepdims=True)
        centered = att - half_mean
        half_sq = jnp.sum(centered * centered, axis=-1, keepdims=True)
        half_g = jnp.sum(g, axis=-1, keepdims=True)
        half_gc = jnp.sum(g * centered, axis=-1, keepdims=True)
        lane = lax.broadcasted_iota(jnp.int32, (SEQ, 128), 1)
        stat_own[...] = jnp.where(
            lane == 0, half_mean, jnp.where(lane == 1, half_sq, jnp.where(lane == 2, half_g, half_gc))
        )
        stat_copy = to_partner(stat_own, stat_other, 2)
        normed_t[...] = normed[...].reshape(SEQ, D).T
    with jax.named_scope("stats_wait"):
        stat_copy.wait_recv()
    with jax.named_scope("norm"):
        other = stat_other[...]
        o_mean, o_sq, o_g, o_gc = (other[:, i : i + 1] for i in range(4))
        mean = 0.5 * (half_mean + o_mean)
        up, o_up = half_mean - mean, o_mean - mean
        var = (half_sq + o_sq + HALF * (up * up + o_up * o_up)) * (1.0 / D)
        rstd = lax.rsqrt(var + EPS)
        mean_g = (half_g + o_g) * (1.0 / D)
        mean_gn = rstd * (half_gc + o_gc + half_g * up + o_g * o_up) * (1.0 / D)
        norm = (att - mean) * rstd
        ng = norm * gain_attn
        mixed = (ng * gating).astype(BF16)
        d_att = (rstd * (g - mean_g - norm * mean_gn) * valid).astype(BF16)
        g_attn = jnp.sum(d_mixed * norm * gating, axis=0, keepdims=True)

    def put(group, halves):
        for half, part in enumerate(halves):
            stream = streams[group + half]
            stream.src[...] = part.astype(BF16).reshape(stream.n[0], stream.n[1], ROWS, 128)
            stream.scatter1()

    def columns_in_halves(t):
        return [t[:, :128], t[:, 128:]]

    def of(group):
        return streams[group : group + 2]

    def weight_grad(g, d_hidden):
        d_pre = (d_hidden * slope[g].reshape(SEQ, HALF)).astype(BF16)
        dpre[g] = d_pre
        return rows_dot(normed_t[...], d_pre)

    with jax.named_scope("grads_u"):
        put(GATING, columns_in_halves(weight_grad(0, d_mixed * ng)))
        g_out = rows_dot(mixed.T, d_proj[...].reshape(SEQ, D))
        pl.semaphore_wait(relay, len(two_away))
        g_out = [g_out[:, i * 128 : i * 128 + 128] for i in range(4)]
        put(OUT, [jnp.concatenate(g_out[:2], axis=0), jnp.concatenate(g_out[2:], axis=0)])
    with jax.named_scope("grads_v"):
        for block in range(2):
            put_heads(d_heads, block, d_att[block * BLK : block * BLK + BLK])
        d_values_0 = sum_rows_dot(weights[0], d_heads[0]) + sum_rows_dot(weights[2], d_heads[1])
        d_values_1 = sum_rows_dot(weights[1], d_heads[1])
        put(VALUES, columns_in_halves(weight_grad(1, jnp.concatenate([d_values_0, d_values_1], axis=0))))
    with jax.named_scope("grads_k"):
        slopes = []
        for tile, (q_block, k_block) in enumerate(((0, 0), (1, 1), (1, 0))):
            slopes.append((cols_dot(d_heads[q_block], hid[1, k_block]) * turn[tile]).astype(BF16))
        d_keys_0 = sum_rows_dot(slopes[0], q_heads[0]) + sum_rows_dot(slopes[2], q_heads[1])
        d_keys_1 = sum_rows_dot(slopes[1], q_heads[1])
        put(KEYS, columns_in_halves(weight_grad(3, jnp.concatenate([d_keys_0, d_keys_1], axis=0))))
    with jax.named_scope("grads_q"):
        d_query_0 = rows_dot(heads_beside(slopes[0]), k_heads[0])
        d_query_1 = rows_dot(heads_beside(slopes[1]), k_heads[1]) + rows_dot(heads_beside(slopes[2]), k_heads[0])
        put(QUERIES, columns_in_halves(weight_grad(2, jnp.concatenate([d_query_0, d_query_1], axis=0))))
    def gains_fan(axis, buf):
        own = buf.at[place.pos[axis]]
        for _, device in place.peers[axis]:
            pltpu.make_async_remote_copy(
                src_ref=own,
                dst_ref=own,
                send_sem=gssem.at[axis],
                recv_sem=grsem.at[axis],
                device_id=device,
                device_id_type=MESH,
            ).start()

    def gains_total(axis, buf):
        n = SIZES[axis]
        wait_bytes(buf.at[pl.ds(0, n - 1)], grsem.at[axis])
        acc = buf[0]
        for j in range(1, n):
            acc = acc + buf[j]
        return acc

    order = of(OUT) + of(GATING) + of(VALUES) + of(KEYS) + of(QUERIES)
    with jax.named_scope("d_norm"):
        d_norm = cols_dot(dpre[0], w_own[0])
        for g in range(1, 4):
            d_norm = d_norm + cols_dot(dpre[g], w_own[g])
        dnorm[...] = d_norm.reshape(2, BLK, D)
        dnorm_copy = to_partner(dnorm.at[away], dnorm_in, 3)
    with jax.named_scope("proj"):
        proj[...] = rows_dot(mixed, wo_own[...]).reshape(2, BLK, D)
        proj_copy = to_partner(proj.at[away], proj_in, 4)

    with jax.named_scope("scatter2_u"):
        for s in of(GATING):
            s.scatter2()
    with jax.named_scope("gain_sums"):
        xhat = xhat_own[...]
        dnorm_copy.wait_recv()
        d_norm = dnorm[core] + dnorm_in[...]
        gain_part = jnp.sum(d_norm * xhat, axis=0, keepdims=True)
        mine = (core == 0).astype(F32)
        gx0_own = gx0.at[core]
        for i in range(4):
            gx0_own[i : i + 1, :] = gain_part[:, i * 128 : i * 128 + 128]
        for i in range(2):
            part = g_attn[:, i * 128 : i * 128 + 128]
            gx0_own[4 + i : 5 + i, :] = part * mine
            gx0_own[6 + i : 7 + i, :] = part * (1.0 - mine)
        gain_copy = to_partner(gx0_own, gx0_own, 5)

    with jax.named_scope("grad_history"):
        e = d_norm * gains[0]
        d_hist = rstd_in * (
            e - jnp.mean(e, axis=-1, keepdims=True) - xhat * jnp.mean(e * xhat, axis=-1, keepdims=True)
        )
        grad_ref[...] = (cots[core].astype(F32) + d_hist).astype(BF16)
        proj_copy.wait_recv()
        out_ref[...] = (hist[...].astype(F32) + valid_rows(core) * (proj[core] + proj_in[...])).astype(BF16)

    with jax.named_scope("scatter2_out"):
        for s in of(OUT):
            s.scatter2()
    with jax.named_scope("gains_x"):
        gain_copy.wait_recv()
        gx1[place.pos[0]] = gx0[0] + gx0[1]
        gains_fan(0, gx1)

    with jax.named_scope("scatter2_rest"):
        for s in of(KEYS) + of(QUERIES) + of(VALUES):
            s.scatter2()
    with jax.named_scope("exchange_first"):
        for s in of(GATING) + of(OUT):
            s.exchange()
    with jax.named_scope("gains_y"):
        gx2[place.pos[1]] = gains_total(0, gx1)
        gains_fan(1, gx2)
    with jax.named_scope("exchange_rest"):
        for s in of(KEYS) + of(VALUES) + of(QUERIES):
            s.exchange()
    with jax.named_scope("gather2_first"):
        for s in of(GATING) + of(OUT):
            s.gather2()
    with jax.named_scope("gains_z"):
        gx3[place.pos[2]] = gains_total(1, gx2)
        gains_fan(2, gx3)
    with jax.named_scope("gather2_rest"):
        for s in of(KEYS) + of(VALUES) + of(QUERIES):
            s.gather2()
    with jax.named_scope("gather1"):
        for s in order:
            s.gather1()
    with jax.named_scope("finish"):
        forwards = []
        for i, s in enumerate(order):
            s.finish()
            forwards.append(
                pltpu.make_async_remote_copy(
                    src_ref=s.res,
                    dst_ref=s.res,
                    send_sem=fssem.at[i],
                    recv_sem=frsem.at[i],
                    device_id=partner,
                    device_id_type=MESH,
                )
            )
            forwards[-1].start()
    with jax.named_scope("gains_end"):
        gains_ref[...] = gains_total(2, gx3)
    with jax.named_scope("drain"):
        for axis, buf in enumerate((gx1, gx2, gx3)):
            wait_bytes(buf.at[pl.ds(0, SIZES[axis] - 1)], gssem.at[axis])
        for copy in (normed_copy, cots_copy, stat_copy, dnorm_copy, proj_copy, gain_copy):
            copy.wait_send()
        for s in streams:
            s.drain()
        for copy in forwards:
            copy.wait()


def widen_kernel(factor, *refs):
    ns = len(STREAMS)
    out_in, grad_in, gains_ref, results = refs[0], refs[1], refs[2], refs[3 : 3 + ns]
    out_ref, grad_ref, w_in_ref, w_out_ref, gin_ref, gattn_ref, w_in_wide, w_out_wide, gains_wide, sem = refs[3 + ns :]
    copies = []

    def send(src, dst):
        copies.append(pltpu.make_async_copy(src, dst, sem.at[len(copies)]))
        copies[-1].start()

    def wide(t):
        return t.astype(F32) * factor

    for half in range(2):
        for core in range(2):
            part = wide(results[OUT + half][core].reshape(D, 128))
            for i in range(2):
                column = (2 * half + i) * 128
                w_out_wide[core * HALF : core * HALF + HALF, column : column + 128] = part[i * HALF : i * HALF + HALF]
    send(w_out_wide, w_out_ref)
    for g in range(4):
        for core in range(2):
            for half in range(2):
                column = (4 * g + 2 * core + half) * 128
                part = results[STREAM_OF[g] + half][core].reshape(D, 128)
                w_in_wide[:, column : column + 128] = wide(part)
            columns = slice((4 * g + 2 * core) * 128, (4 * g + 2 * core + 2) * 128)
            send(w_in_wide.at[:, columns], w_in_ref.at[:, columns])
    for i in range(4):
        gains_wide[0, :, i * 128 : i * 128 + 128] = gains_ref[i : i + 1, :] * factor
        gains_wide[1, :, i * 128 : i * 128 + 128] = gains_ref[4 + i : 5 + i, :] * factor
    send(gains_wide.at[0], gin_ref)
    send(gains_wide.at[1], gattn_ref)
    send(out_in, out_ref)
    send(grad_in, grad_ref)
    for copy in copies:
        copy.wait()


VMEM = pl.BlockSpec(memory_space=pltpu.VMEM)
SMEM = pl.BlockSpec(memory_space=pltpu.SMEM)
HBM = pl.BlockSpec(memory_space=pltpu.HBM)


def shape(dims, kind):
    return jax.ShapeDtypeStruct(dims, kind)


def per_device(users, history, lengths, input_gain, gain_attn, w_in, w_out, cotangent):
    history, cotangent = history[0], cotangent[0]
    input_gain, gain_attn = input_gain[None], gain_attn[None]
    operands = [history, cotangent, input_gain, gain_attn, w_in, w_out]
    operands = [pltpu.with_memory_space_constraint(t, pltpu.HBM) for t in operands]
    dma = pltpu.SemaphoreType.DMA

    buffers, result_shapes = [], []
    for order in STREAMS:
        n = [SIZES[a] for a in order]
        result_shapes.append(shape((2, n[0], n[1], ROWS, 128), BF16))
        buffers += [
            pltpu.VMEM((n[0], n[1], ROWS, 128), BF16),
            pltpu.VMEM((n[0], n[1], ROWS, 128), BF16),
            pltpu.VMEM((n[1], ROWS, 128), BF16),
            pltpu.VMEM((n[1], ROWS, 128), BF16),
            pltpu.VMEM((n[2], ROWS, 128), BF16),
        ]
    ns = len(STREAMS)
    heads = pltpu.VMEM((2, HEADS * BLK, HALF), BF16)
    out, grad, gains, *results = pl.pallas_call(
        layer_kernel,
        out_shape=(shape((BLK, D), BF16), shape((BLK, D), BF16), shape((8, 128), F32), *result_shapes),
        in_specs=[SMEM] + [HBM] * 6,
        out_specs=(VMEM,) * (3 + ns),
        scratch_shapes=buffers
        + [
            pltpu.VMEM((BLK, D), BF16),
            pltpu.VMEM((2, 1, D), F32),
            pltpu.VMEM((2, BLK, D), BF16),
            pltpu.VMEM((2, BLK, D), BF16),
            pltpu.VMEM((D, SEQ), BF16),
            pltpu.VMEM((BLK, D), F32),
            pltpu.VMEM((4, D, HALF), BF16),
            pltpu.VMEM((HALF, D), BF16),
            pltpu.VMEM((4, 2, BLK, HALF), BF16),
            pltpu.VMEM((4, 2, BLK, HALF), F32),
            heads,
            heads,
            heads,
            heads,
            pltpu.VMEM((3, HEADS * BLK, BLK), BF16),
            pltpu.VMEM((3, HEADS * BLK, BLK), F32),
            pltpu.VMEM((2, BLK, HALF), F32),
            pltpu.VMEM((2, BLK, D), BF16),
            pltpu.VMEM((2, BLK, HALF), F32),
            pltpu.VMEM((4, SEQ, HALF), BF16),
            pltpu.VMEM((SEQ, 128), F32),
            pltpu.VMEM((SEQ, 128), F32),
            pltpu.VMEM((2, BLK, D), F32),
            pltpu.VMEM((BLK, D), F32),
            pltpu.VMEM((2, BLK, D), F32),
            pltpu.VMEM((BLK, D), F32),
            pltpu.VMEM((2, 8, 128), F32),
            pltpu.VMEM((4, 8, 128), F32),
            pltpu.VMEM((8, 8, 128), F32),
            pltpu.VMEM((8, 8, 128), F32),
            dma((9,)),
            dma((LEVELS * ns,)),
            dma((LEVELS * ns,)),
            dma((6,)),
            dma((6,)),
            dma((3,)),
            dma((3,)),
            dma((ns,)),
            dma((ns,)),
            pltpu.SemaphoreType.REGULAR,
        ],
        compiler_params=pltpu.CompilerParams(collective_id=1, has_side_effects=True, vmem_limit_bytes=48 << 20),
        name="layer",
    )(lengths, *operands)

    factor = 1.0 / math.sqrt(users * SEQ)
    out, grad, g_in, g_out, gain_in_grad, gain_attn_grad = pl.pallas_call(
        functools.partial(widen_kernel, factor),
        out_shape=(
            shape((BLK, D), BF16),
            shape((BLK, D), BF16),
            shape((D, 4 * D), F32),
            shape((D, D), F32),
            shape((1, D), F32),
            shape((1, D), F32),
        ),
        in_specs=[VMEM] * (3 + ns),
        out_specs=(HBM,) * 6,
        scratch_shapes=[
            pltpu.VMEM((D, 4 * D), F32),
            pltpu.VMEM((D, D), F32),
            pltpu.VMEM((2, 1, D), F32),
            dma((13,)),
        ],
        compiler_params=pltpu.CompilerParams(vmem_limit_bytes=32 << 20),
        name="widen",
    )(out, grad, gains, *results)
    return out[None], grad[None], g_in, g_out, gain_in_grad[0], gain_attn_grad[0]


def solution(mesh):
    placed = (P("dp", "ctx", None), P("dp"), P(), P(), P(), P(), P("dp", "ctx", None))
    return jax.shard_map(
        functools.partial(per_device, mesh.shape["dp"]),
        mesh=mesh,
        in_specs=placed,
        out_specs=(P("dp", "ctx", None), P("dp", "ctx", None), P(), P(), P(), P()),
        check_vma=False,
    )
```
